32 devices in a mesh: dp: 8 (over z, x), tensor: 4 (over y, core).
Axes of the slice: x: 2, y: 2, z: 4, core: 2. Of those that a mesh axis runs over, the one named last changes fastest.
Arguments:
- tokens: bfloat16 [4096, 1024], P(('dp', 'tensor')), may hold values from -6 to 6
- lengths: int32 [8, 2], P('dp'), may hold values from 1 to 448, as said below
- cotangent: bfloat16 [4096, 1024], P(('dp', 'tensor')), may hold values from -6 to 6
- norm_gain: bfloat16 [1024], P('dp'), may hold values from 0.5 to 1.5
- query_weight: bfloat16 [1024, 1024], P('dp', 'tensor'), may hold values from -0.1875 to 0.1875
- key_weight: bfloat16 [1024, 1024], P('dp', 'tensor'), may hold values from -0.1875 to 0.1875
- value_weight: bfloat16 [1024, 2048], P('dp', 'tensor'), may hold values from -0.1875 to 0.1875
- gate_weight: bfloat16 [1024, 2048], P('dp', 'tensor'), may hold values from -0.1875 to 0.1875
- beta_weight: bfloat16 [1024, 4], P('dp', 'tensor'), may hold values from -0.1875 to 0.1875
- decay_weight: bfloat16 [1024, 4], P('dp', 'tensor'), may hold values from -0.1875 to 0.1875
- query_conv: bfloat16 [4, 1024], P(None, ('tensor', 'dp')), may hold values from -2.5 to 2.5
- key_conv: bfloat16 [4, 1024], P(None, ('tensor', 'dp')), may hold values from -2.5 to 2.5
- value_conv: bfloat16 [4, 2048], P(None, ('tensor', 'dp')), may hold values from -2.5 to 2.5
- decay_params: float32 [2, 4], P(None, 'tensor'), may hold values from -4 to 0
- head_gain: bfloat16 [2048], P(('tensor', 'dp')), may hold values from 0.5 to 1.5
- out_weight: bfloat16 [2048, 1024], P('tensor', 'dp'), may hold values from -0.1875 to 0.1875
- ffn_gain: bfloat16 [1024], P('dp'), may hold values from 0.5 to 1.5
- ffn_gate: bfloat16 [1024, 2816], P('dp', 'tensor'), may hold values from -0.1875 to 0.1875
- ffn_up: bfloat16 [1024, 2816], P('dp', 'tensor'), may hold values from -0.1875 to 0.1875
- ffn_down: bfloat16 [2816, 1024], P('tensor', 'dp'), may hold values from -0.15625 to 0.15625
Outputs:
- block_out: bfloat16 [4096, 1024], P(('dp', 'tensor'))
- tokens_grad: float32 [4096, 1024], P(('dp', 'tensor'))
- norm_gain_grad: float32 [1024], P('dp')
- query_weight_grad: float32 [1024, 1024], P('dp', 'tensor')
- key_weight_grad: float32 [1024, 1024], P('dp', 'tensor')
- value_weight_grad: float32 [1024, 2048], P('dp', 'tensor')
- gate_weight_grad: float32 [1024, 2048], P('dp', 'tensor')
- beta_weight_grad: float32 [1024, 4], P('dp', 'tensor')
- decay_weight_grad: float32 [1024, 4], P('dp', 'tensor')
- query_conv_grad: float32 [4, 1024], P(None, ('tensor', 'dp'))
- key_conv_grad: float32 [4, 1024], P(None, ('tensor', 'dp'))
- value_conv_grad: float32 [4, 2048], P(None, ('tensor', 'dp'))
- decay_params_grad: float32 [2, 4], P(None, 'tensor')
- head_gain_grad: float32 [2048], P(('tensor', 'dp'))
- out_weight_grad: float32 [2048, 1024], P('tensor', 'dp')
- ffn_gain_grad: float32 [1024], P('dp')
- ffn_gate_grad: float32 [1024, 2816], P('dp', 'tensor')
- ffn_up_grad: float32 [1024, 2816], P('dp', 'tensor')
- ffn_down_grad: float32 [2816, 1024], P('tensor', 'dp')
The draws below stay inside these ranges and needn't reach their ends.
Inputs may be any that keep to these rules, and one draw needn't show every extreme that they name: `lengths`: each group holds two sequences; one fills 8 - 1 blocks after padding, the other one block, in either order; group 0's longer sequence has no padding.
All inputs are finite; a program needn't handle non-finite values.
Results may differ from the reference program's by a relative error of at most 0.014.
Values may be sent and summed in bfloat16 or wider, within the bound.
No kernel may reach another device: no remote copies, remote signals or barrier semaphores. Data moves between devices by JAX's collectives and lax.ppermute only.
A program may use at most 128 MiB of HBM per device.

```python
import math
import jax
import jax.numpy as jnp
from jax import lax

D = 1024
H = 4
DK = 256
DV = 512
FF = 2816
CONV = 4
BLOCK = 64
GROUP_TOK = 512
QK = 1024
VW = 2048
TOKENS = 4096


def draw_lengths(key, part):
    key = jax.random.fold_in(key, 7)
    groups = TOKENS // GROUP_TOK
    blocks = GROUP_TOK // BLOCK
    order_key, long_key, short_key = jax.random.split(key, 3)
    long_first = jax.random.randint(order_key, (groups,), 0, 2)
    long_len = (blocks - 1) * BLOCK - jax.random.randint(long_key, (groups,), 0, BLOCK // 2)
    long_len = jnp.where(jnp.arange(groups) == 0, (blocks - 1) * BLOCK, long_len)
    short_len = jax.random.randint(short_key, (groups,), 1, BLOCK + 1)
    first_len = jnp.where(long_first == 1, long_len, short_len)
    second_len = jnp.where(long_first == 1, short_len, long_len)
    return jnp.stack([first_len, second_len], axis=1).astype(jnp.int32)


def draw_decay_params(key, part):
    key = jax.random.fold_in(key, 11)
    rate_key, bias_key = jax.random.split(key)
    rates = jax.random.uniform(rate_key, (H,), jnp.float32, math.log(0.02), 0.0)
    biases = jax.random.uniform(bias_key, (H,), jnp.float32, -3.0, -0.5)
    return jnp.stack([rates, biases]).astype(jnp.float32)


def levels(rng, shape, cuts, smallest, top_value):
    def one(axis_at, parts):
        steps = jax.random.uniform(jax.random.fold_in(jax.random.fold_in(rng, 6), axis_at), (parts,), jnp.float32, smallest / len(cuts), top_value / len(cuts))
        return jnp.repeat(jnp.exp(steps), shape[axis_at] // parts).reshape((-1,) + (1,) * (len(shape) - axis_at - 1))

    loudness = one(*cuts[0])
    for cut in cuts[1:]:
        loudness = loudness * one(*cut)
    return loudness


def noise(own_key, extent, scale, limit, shards=(), held_as=jnp.bfloat16):
    drawn = jax.random.normal(own_key, extent, jnp.float32) * scale
    if len(shards) > 0:
        drawn = levels(own_key, extent, shards, -0.22, 0.18) * drawn
    return jnp.clip(drawn, min=-limit, max=limit).astype(held_as)


def setup_inputs(seed: int = 0) -> dict:
    streams_of = jax.random.split(jax.random.key(seed), 21)
    tokens = noise(streams_of[0], (TOKENS, D), 1.0, 6.0, ((0, 32),))
    lengths = draw_lengths(jax.random.fold_in(streams_of[20], 71), 0)
    cotangent = noise(streams_of[2], (TOKENS, D), 1.0, 6.0, ((0, 32),))
    norm_gain = jnp.clip(1.0 + 0.1 * jax.random.normal(streams_of[3], (D,), jnp.float32), 0.5, 1.5).astype(jnp.bfloat16)
    query_weight = noise(streams_of[4], (D, QK), D ** -0.5, 0.1875, ((0, 8), (1, 4)))
    key_weight = noise(streams_of[5], (D, QK), D ** -0.5, 0.1875, ((0, 8), (1, 4)))
    value_weight = noise(streams_of[6], (D, VW), D ** -0.5, 0.1875, ((0, 8), (1, 4)))
    gate_weight = noise(streams_of[7], (D, VW), D ** -0.5, 0.1875, ((0, 8), (1, 4)))
    beta_weight = noise(streams_of[8], (D, H), D ** -0.5, 0.1875, ((0, 8), (1, 4)))
    decay_weight = noise(streams_of[9], (D, H), D ** -0.5, 0.1875, ((0, 8), (1, 4)))
    query_conv = noise(streams_of[10], (CONV, QK), 0.5, 2.5, ((1, 32),))
    key_conv = noise(streams_of[11], (CONV, QK), 0.5, 2.5, ((1, 32),))
    value_conv = noise(streams_of[12], (CONV, VW), 0.5, 2.5, ((1, 32),))
    decay_params = draw_decay_params(jax.random.fold_in(streams_of[20], 71), 0)
    head_gain = jnp.clip(1.0 + 0.1 * jax.random.normal(streams_of[14], (VW,), jnp.float32), 0.5, 1.5).astype(jnp.bfloat16)
    out_weight = noise(streams_of[15], (VW, D), (VW // 2) ** -0.5, 0.1875, ((0, 4), (1, 8)))
    ffn_gain = jnp.clip(1.0 + 0.1 * jax.random.normal(streams_of[16], (D,), jnp.float32), 0.5, 1.5).astype(jnp.bfloat16)
    ffn_gate = noise(streams_of[17], (D, FF), D ** -0.5, 0.1875, ((0, 8), (1, 4)))
    ffn_up = noise(streams_of[18], (D, FF), D ** -0.5, 0.1875, ((0, 8), (1, 4)))
    ffn_down = noise(streams_of[19], (FF, D), (FF // 2) ** -0.5, 0.15625, ((0, 4), (1, 8)))
    return {"tokens": tokens, "lengths": lengths, "cotangent": cotangent, "norm_gain": norm_gain, "query_weight": query_weight, "key_weight": key_weight, "value_weight": value_weight, "gate_weight": gate_weight, "beta_weight": beta_weight, "decay_weight": decay_weight, "query_conv": query_conv, "key_conv": key_conv, "value_conv": value_conv, "decay_params": decay_params, "head_gain": head_gain, "out_weight": out_weight, "ffn_gain": ffn_gain, "ffn_gate": ffn_gate, "ffn_up": ffn_up, "ffn_down": ffn_down}


HIGHEST = lax.Precision.HIGHEST

@jax.custom_vjp
def low(v):
    return lax.optimization_barrier(v.astype(jnp.bfloat16)).astype(jnp.float32)

@jax.custom_vjp
def low_back(v):
    return v

def low_keep(v):
    return (low(v), None)

def low_pass(kept, grad):
    return (grad,)

def back_keep(v):
    return (v, None)

def back_low(kept, grad):
    return (low(grad),)
low.defvjp(low_keep, low_pass)
low_back.defvjp(back_keep, back_low)

def both_ways(value):
    return low_back(low(value))

def rms_scale(value, gain):
    return low(value * lax.rsqrt(lax.optimization_barrier(jnp.mean(value * value, axis=-1, keepdims=True)) + 1e-06) * gain)

def full_product(left, right):
    return jnp.dot(left, right, precision=HIGHEST)

def group_layout(lengths_row, total, dtype):
    first_len = lengths_row[0]
    second_len = lengths_row[1]
    start = (first_len + BLOCK - 1) // BLOCK * BLOCK
    place = jnp.arange(total, dtype=jnp.int32)
    later = place >= start
    segment = later.astype(jnp.int32)
    valid = jnp.where(later, place - start < second_len, place < first_len).astype(dtype)
    block_starts = jnp.arange(total // BLOCK, dtype=jnp.int32) * BLOCK
    reset = ((block_starts == 0) | (block_starts == start)).astype(dtype)
    return (segment, valid, reset)

def causal_conv(proj, taps, segment):
    total = proj.shape[0]
    result = proj * taps[0]
    for offset in range(1, taps.shape[0]):
        shifted = jnp.concatenate([jnp.zeros((offset, proj.shape[1]), proj.dtype), proj[:total - offset]], axis=0)
        same = jnp.concatenate([jnp.zeros((offset,), jnp.bool_), segment[offset:] == segment[:total - offset]])
        result = result + jnp.where(same[:, None], shifted, 0.0) * taps[offset]
    return result

def unit_lower_inverse(coupling):
    size = coupling.shape[-1]
    rows = lax.broadcasted_iota(jnp.int32, (size, size), 0)
    cols = lax.broadcasted_iota(jnp.int32, (size, size), 1)
    inverse = jnp.broadcast_to(jnp.eye(size, dtype=coupling.dtype), coupling.shape)
    width = 1
    while width < size:
        inner = (rows // (2 * width) == cols // (2 * width)) & (rows // width != cols // width)
        lower_part = jnp.where(inner, coupling, 0.0)
        inverse = inverse - jnp.einsum('hij,hjk,hkl->hil', inverse, lower_part, inverse, precision=HIGHEST)
        width = width * 2
    return inverse

def block_step(state, items):
    query, key, value, beta, logdecay, reset = items
    state = state * (1.0 - reset)
    size = query.shape[0]
    rows = lax.broadcasted_iota(jnp.int32, (size, size), 0)
    cols = lax.broadcasted_iota(jnp.int32, (size, size), 1)
    causal = rows >= cols
    strict = rows > cols
    running = jnp.cumsum(logdecay, axis=0)
    spread = running.T[:, :, None] - running.T[:, None, :]
    ratio = jnp.where(causal, jnp.exp(jnp.where(causal, spread, 0.0)), 0.0)
    intersection = jnp.einsum('ihd,jhd->hij', key, key, precision=HIGHEST)
    coupling = jnp.where(strict, beta.T[:, :, None] * intersection * ratio, 0.0)
    inverse = unit_lower_inverse(coupling)
    growth = jnp.exp(running)
    right = jnp.concatenate([beta[:, :, None] * value, (beta * growth)[:, :, None] * key], axis=2)
    solved = jnp.einsum('hij,jhe->ihe', inverse, right, precision=HIGHEST)
    width = value.shape[2]
    fresh = solved[:, :, :width] - jnp.einsum('ihd,hde->ihe', solved[:, :, width:], state, precision=HIGHEST)
    scores = jnp.einsum('ihd,jhd->hij', query, key, precision=HIGHEST) * ratio
    output = jnp.einsum('ihd,hde->ihe', query * growth[:, :, None], state, precision=HIGHEST)
    output = output + jnp.einsum('hij,jhe->ihe', scores, fresh, precision=HIGHEST)
    final = running[-1]
    tail = jnp.exp(final[None, :] - running)
    state = jnp.exp(final)[:, None, None] * state + jnp.einsum('jhd,jhe->hde', key * tail[:, :, None], fresh, precision=HIGHEST)
    return (state, output)

def mixer_core(query_proj, key_proj, value_proj, gate_proj, beta_proj, decay_proj, query_conv, key_conv, value_conv, decay_params, head_gain, lengths_row):
    total = query_proj.shape[0]
    heads = beta_proj.shape[1]
    segment, valid, reset = group_layout(lengths_row, total, query_proj.dtype)
    query = jax.nn.silu(causal_conv(query_proj, query_conv, segment)).reshape(total, heads, DK)
    key = jax.nn.silu(causal_conv(key_proj, key_conv, segment)).reshape(total, heads, DK)
    value = jax.nn.silu(causal_conv(value_proj, value_conv, segment)).reshape(total, heads, DV)
    query = both_ways(query * lax.rsqrt(lax.optimization_barrier(jnp.sum(query * query, axis=2, keepdims=True)) + 1e-06) * DK ** (-0.5))
    key = both_ways(key * lax.rsqrt(lax.optimization_barrier(jnp.sum(key * key, axis=2, keepdims=True)) + 1e-06))
    value = both_ways(value)
    beta = jax.nn.sigmoid(beta_proj)
    logdecay = -jnp.exp(decay_params[0]) * jax.nn.softplus(decay_proj + decay_params[1])
    blocks = total // BLOCK

    def into_blocks(piece):
        return piece.reshape((blocks, BLOCK) + piece.shape[1:])
    start_state = jnp.zeros((heads, DK, DV), query_proj.dtype)
    carried, mixed = lax.scan(block_step, start_state, (into_blocks(query), into_blocks(key), into_blocks(value), into_blocks(beta), into_blocks(logdecay), reset))
    mixed = mixed.reshape(total, heads, DV) * valid[:, None, None]
    normed = mixed * lax.rsqrt(lax.optimization_barrier(jnp.mean(mixed * mixed, axis=2, keepdims=True)) + 1e-06) * head_gain.reshape(heads, DV)
    return low(normed.reshape(total, heads * DV) * jax.nn.silu(gate_proj))

def forward(token_rows, norm_gain, query_weight, key_weight, value_weight, gate_weight, beta_weight, decay_weight, query_conv, key_conv, value_conv, decay_params, head_gain, out_weight, ffn_gain, ffn_gate, ffn_up, ffn_down, lengths):
    first = rms_scale(token_rows, norm_gain)
    query_proj = low_back(full_product(first, query_weight))
    key_proj = low_back(full_product(first, key_weight))
    value_proj = low_back(full_product(first, value_weight))
    gate_proj = low_back(full_product(first, gate_weight))
    beta_proj = low_back(full_product(first, beta_weight))
    decay_proj = low_back(full_product(first, decay_weight))
    groups = lengths.shape[0]

    def regroup(piece):
        return piece.reshape((groups, GROUP_TOK) + piece.shape[1:])

    def one_group(items):
        return mixer_core(items[0], items[1], items[2], items[3], items[4], items[5], query_conv, key_conv, value_conv, decay_params, head_gain, items[6])
    gated = lax.map(jax.checkpoint(one_group), (regroup(query_proj), regroup(key_proj), regroup(value_proj), regroup(gate_proj), regroup(beta_proj), regroup(decay_proj), lengths))
    gated = gated.reshape(token_rows.shape[0], gated.shape[-1])
    middle = token_rows + low_back(full_product(gated, out_weight))
    second = rms_scale(middle, ffn_gain)
    gate_act = low_back(full_product(second, ffn_gate))
    up_act = low_back(full_product(second, ffn_up))
    product = low(jax.nn.silu(gate_act) * up_act)
    return middle + low_back(full_product(product, ffn_down))

def reference(tokens, lengths, cotangent, norm_gain, query_weight, key_weight, value_weight, gate_weight, beta_weight, decay_weight, query_conv, key_conv, value_conv, decay_params, head_gain, out_weight, ffn_gain, ffn_gate, ffn_up, ffn_down):
    params = (tokens, norm_gain, query_weight, key_weight, value_weight, gate_weight, beta_weight, decay_weight, query_conv, key_conv, value_conv, decay_params, head_gain, out_weight, ffn_gain, ffn_gate, ffn_up, ffn_down)
    widened = tuple((piece.astype(jnp.float32) for piece in params))

    def wrapped(*pieces):
        return forward(*pieces, lengths)
    result, pull = jax.vjp(wrapped, *widened)
    grads = pull(cotangent.astype(jnp.float32))
    return (result.astype(jnp.bfloat16), grads[0], grads[1], grads[2], grads[3], grads[4], grads[5], grads[6], grads[7], grads[8], grads[9], grads[10], grads[11], grads[12], grads[13], grads[14], grads[15], grads[16], grads[17])
```

```python
import jax
import jax.numpy as jnp
from jax import lax
from jax.experimental import pallas as pl
from jax.experimental.pallas import tpu as pltpu
from jax.sharding import PartitionSpec as P

DK = 256
DV = 512
BLOCK = 64
SPAN = 256
PART = 128
TOTAL = 512
FRONT = 2 * DK + DV
WIDE = FRONT + 128
BLOCKS = TOTAL // BLOCK
SPANS = TOTAL // SPAN
F32 = jnp.float32
BF16 = jnp.bfloat16
SMEM = pltpu.SMEM
VMEM = pltpu.VMEM
LIMIT = 56 * 1024 * 1024


def mul(left, right):
    return lax.dot_general(left, right, (((1,), (0,)), ((), ())), preferred_element_type=F32)


def mul_nt(left, right):
    return lax.dot_general(left, right, (((1,), (1,)), ((), ())), preferred_element_type=F32)


def mul_tn(left, right):
    return lax.dot_general(left, right, (((0,), (0,)), ((), ())), preferred_element_type=F32)


def low(value):
    return value.astype(BF16)


def halves(value):
    high = low(value)
    return high, low(value - high.astype(F32))


def mul_fine(left, right):
    left_high, left_low = halves(left)
    right_high, right_low = halves(right)
    return mul(left_high, right_high) + (mul(left_high, right_low) + mul(left_low, right_high))


def sigmoid(value):
    return 1.0 / (1.0 + jnp.exp(-value))


def softplus(value):
    return jnp.maximum(value, 0.0) + jnp.log1p(jnp.exp(-jnp.abs(value)))


def span_masks():
    rows = lax.broadcasted_iota(jnp.int32, (SPAN, SPAN), 0)
    cols = lax.broadcasted_iota(jnp.int32, (SPAN, SPAN), 1)
    same = (rows // BLOCK) == (cols // BLOCK)
    return rows, cols, same


def decay_terms(raw, rate, bias, masks):
    rows, cols, same = masks
    causal = same & (rows >= cols)
    column = -jnp.exp(rate) * softplus(raw + bias)
    line = jnp.sum(jnp.where(rows == cols, column, 0.0), axis=0, keepdims=True)
    running = jnp.sum(jnp.where(causal, line, 0.0), axis=1, keepdims=True)
    running_line = jnp.sum(jnp.where(same & (rows <= cols), column, 0.0), axis=0, keepdims=True)
    final = jnp.sum(jnp.where(same, line, 0.0), axis=1, keepdims=True)
    ratio = jnp.where(causal, jnp.exp(jnp.where(causal, running - running_line, 0.0)), 0.0)
    return column, running, final, ratio


def unit_inverse(coupling, masks):
    rows, cols, same = masks
    inverse = jnp.where(rows == cols, 1.0, 0.0) - jnp.where(
        (rows // 2 == cols // 2), coupling, 0.0
    )
    width = 2
    while width < BLOCK:
        inner = (rows // (2 * width) == cols // (2 * width)) & (rows // width != cols // width)
        part = jnp.where(inner, coupling, 0.0)
        inverse = inverse - mul_fine(mul_fine(inverse, part), inverse)
        width = width * 2
    return inverse


def second_start(lengths_ref):
    return (lengths_ref[0, 0] + BLOCK - 1) // BLOCK * BLOCK


def held_rows(order_ref, index):
    half = index % 2
    return pl.multiple_of(order_ref[index // 2] * PART + half * BLOCK, BLOCK)


def part_rows(order_ref, index):
    return pl.ds(pl.multiple_of(order_ref[index] * PART, PART), PART)


def past_rows(order_ref, index):
    return pl.multiple_of(held_rows(order_ref, jnp.maximum(index - 1, 0)) + BLOCK - 8, 8)


def row_limit(lengths_ref, start, base, count):
    place = lax.broadcasted_iota(jnp.int32, (count, 1), 0) + base
    limit = jnp.where(place >= start, start + lengths_ref[0, 1], lengths_ref[0, 0])
    return place < limit


def front_kernel(
    lengths_ref,
    order_ref,
    rates_ref,
    proj_ref,
    taps_ref,
    query_ref,
    key_ref,
    value_ref,
    raw_ref,
    inverse_ref,
    reach_ref,
    base_ref,
    tail_ref,
    score_ref,
    growth_ref,
):
    start = second_start(lengths_ref)
    rate = rates_ref[0, 0]
    bias = rates_ref[1, 0]

    def front(index, carry):
        base = pl.multiple_of(index * BLOCK, BLOCK)
        held = held_rows(order_ref, index)
        before = past_rows(order_ref, index)
        broken = (base == 0) | (base == start)
        raw_ref[pl.ds(base, BLOCK), :] = proj_ref[pl.ds(held, BLOCK), FRONT:WIDE]
        for at in range(0, FRONT, DK):
            here = slice(at, at + DK)
            taps = taps_ref[:, here]
            halo = jnp.where(broken, 0.0, proj_ref[pl.ds(before, 8), here])
            block = proj_ref[pl.ds(held, BLOCK), here]
            joined = jnp.concatenate([halo, block], axis=0)
            conv = block * taps[0:1]
            for offset in range(1, 4):
                conv = conv + pltpu.roll(joined, offset, 0)[8:] * taps[offset : offset + 1]
            act = conv * sigmoid(conv)
            if at >= 2 * DK:
                value_ref[pl.ds(base, BLOCK), at - 2 * DK : at - DK] = low(act)
            else:
                inv = lax.rsqrt(jnp.sum(act * act, axis=1, keepdims=True) + 1e-06)
                if at == 0:
                    query_ref[pl.ds(base, BLOCK), :] = low(act * inv * DK ** (-0.5))
                else:
                    key_ref[pl.ds(base, BLOCK), :] = low(act * inv)
        return carry

    lax.fori_loop(0, BLOCKS, front, 0)

    masks = span_masks()
    rows, cols, same = masks
    strict = same & (rows > cols)
    lane = lax.broadcasted_iota(jnp.int32, (SPAN, 128), 1)
    for span in range(SPANS):
        at = slice(span * SPAN, (span + 1) * SPAN)
        raw = raw_ref[at, :]
        beta = sigmoid(raw[:, 0:1])
        _, running, final, ratio = decay_terms(raw[:, 1:2], rate, bias, masks)
        growth = jnp.exp(running)
        key = key_ref[at, :]
        coupling = jnp.where(strict, beta * mul_nt(key, key) * ratio, 0.0)
        inverse = low(unit_inverse(coupling, masks))
        inverse_ref[at, :] = inverse
        key_wide = key.astype(F32)
        base_ref[at, :] = mul(inverse, low(beta * value_ref[at, :].astype(F32)))
        reach_ref[at, :] = low(mul(inverse, low(beta * growth * key_wide)))
        tail_ref[at, :] = low(jnp.exp(final - running) * key_wide)
        score_ref[at, :] = low(mul_nt(query_ref[at, :], key) * ratio)
        growth_ref[at, :] = jnp.where(lane == 0, growth, jnp.exp(final))


def chain_kernel(
    lengths_ref,
    order_ref,
    query_ref,
    reach_ref,
    base_ref,
    tail_ref,
    score_ref,
    growth_ref,
    gate_ref,
    gain_ref,
    gated_ref,
    state_ref,
    fresh_ref,
    out_ref,
    carry_ref,
):
    start = second_start(lengths_ref)
    carry_ref[...] = jnp.zeros_like(carry_ref)
    for index in range(BLOCKS):
        at = slice(index * BLOCK, (index + 1) * BLOCK)
        held = jnp.where(start == index * BLOCK, 0.0, carry_ref[...])
        state = low(held)
        state_ref[index] = state
        both = mul(jnp.concatenate([reach_ref[at, :], query_ref[at, :]], axis=0), state)
        fresh = low(base_ref[at, :] - both[:BLOCK])
        fresh_ref[at, :] = fresh
        out_ref[at, :] = growth_ref[at, 0:1] * both[BLOCK:]
        if index + 1 < BLOCKS:
            final = growth_ref[index * BLOCK : index * BLOCK + 1, 1:2]
            carry_ref[...] = final * held + mul_tn(tail_ref[at, :], fresh)

    gain = gain_ref[...]
    for part in range(TOTAL // PART):
        span = part * PART // SPAN
        here = slice(part * PART, (part + 1) * PART)
        out = out_ref[here, :] + mul(score_ref[here, :], fresh_ref[span * SPAN : (span + 1) * SPAN, :])
        out = jnp.where(row_limit(lengths_ref, start, part * PART, PART), out, 0.0)
        out_ref[here, :] = out
        inv = lax.rsqrt(jnp.mean(out * out, axis=1, keepdims=True) + 1e-06)
        held = part_rows(order_ref, part)
        gate = gate_ref[held, :]
        gated_ref[held, :] = low(out * inv * gain * (gate * sigmoid(gate)))


def gate_back_kernel(
    lengths_ref,
    order_ref,
    grad_ref,
    gate_ref,
    gain_ref,
    out_ref,
    dgate_ref,
    dout_ref,
    dgain_ref,
):
    start = second_start(lengths_ref)
    gain = gain_ref[...]
    dgain = jnp.zeros((1, DV), F32)
    for part in range(TOTAL // PART):
        here = slice(part * PART, (part + 1) * PART)
        held = part_rows(order_ref, part)
        out = out_ref[here, :]
        gate = gate_ref[held, :]
        grad = grad_ref[held, :]
        inv = lax.rsqrt(jnp.mean(out * out, axis=1, keepdims=True) + 1e-06)
        sig = sigmoid(gate)
        swish = gate * sig
        unit = out * inv
        pulled = grad * unit
        dgate_ref[held, :] = low(pulled * gain * (sig * (1.0 + gate * (1.0 - sig))))
        dgain = dgain + jnp.sum(pulled * swish, axis=0, keepdims=True)
        inner = grad * swish * gain
        dout = inv * (inner - unit * jnp.mean(inner * unit, axis=1, keepdims=True))
        dout_ref[here, :] = low(
            jnp.where(row_limit(lengths_ref, start, part * PART, PART), dout, 0.0)
        )
    dgain_ref[...] = dgain


def back_kernel(
    lengths_ref,
    order_ref,
    rates_ref,
    proj_ref,
    taps_ref,
    dout_ref,
    raw_ref,
    query_ref,
    key_ref,
    value_ref,
    state_ref,
    inverse_ref,
    reach_ref,
    fresh_ref,
    dproj_ref,
    dtaps_ref,
    drates_ref,
    dfresh_ref,
    dstate_ref,
    carry_ref,
    dq_ref,
    dk_ref,
    dv_ref,
    halo_ref,
):
    start = second_start(lengths_ref)
    rate = rates_ref[0, 0]
    bias = rates_ref[1, 0]
    masks = span_masks()
    rows, cols, same = masks
    causal = same & (rows >= cols)
    strict = same & (rows > cols)

    kept = []
    for span in range(SPANS):
        at = slice(span * SPAN, (span + 1) * SPAN)
        dout = dout_ref[at, :]
        raw = raw_ref[at, :]
        beta = sigmoid(raw[:, 0:1])
        column, running, final, ratio = decay_terms(raw[:, 1:2], rate, bias, masks)
        growth = jnp.exp(running)
        tail = jnp.exp(final - running)
        key = key_ref[at, :]
        score = mul_nt(query_ref[at, :], key) * ratio
        dfresh_ref[at, :] = mul_tn(low(score), dout)
        dscore = jnp.where(causal, mul_nt(dout, fresh_ref[at, :]), 0.0)
        tailed = low(tail * key.astype(F32))
        kept.append((beta, column, growth, final, tail, ratio, score, dscore, tailed))

    carry_ref[...] = jnp.zeros_like(carry_ref)
    ends = [None] * BLOCKS
    for index in reversed(range(BLOCKS)):
        at = slice(index * BLOCK, (index + 1) * BLOCK)
        low_at = index * BLOCK % SPAN
        inner = slice(low_at, low_at + BLOCK)
        beta, column, growth, final, tail, ratio, score, dscore, tailed = kept[index * BLOCK // SPAN]
        held = carry_ref[...]
        dstate = low(held)
        dstate_ref[index] = dstate
        dfresh = low(dfresh_ref[at, :] + mul(tailed[inner], dstate))
        dfresh_ref[at, :] = dfresh.astype(F32)
        scale = jnp.exp(final[low_at : low_at + 1])
        if index > 0:
            left = jnp.concatenate(
                [low(query_ref[at, :].astype(F32) * growth[inner]), -reach_ref[at, :]], axis=0
            )
            right = jnp.concatenate([dout_ref[at, :], dfresh], axis=0)
            carry_ref[...] = jnp.where(
                start == index * BLOCK, 0.0, scale * held + mul_tn(left, right)
            )
        ends[index] = scale * jnp.sum(
            jnp.sum(held * state_ref[index].astype(F32), axis=0, keepdims=True), axis=1, keepdims=True
        )

    drate = jnp.zeros((1, 1), F32)
    dbias = jnp.zeros((1, 1), F32)
    steps = SPAN // BLOCK
    for span in range(SPANS):
        at = slice(span * SPAN, (span + 1) * SPAN)
        beta, column, growth, final, tail, ratio, score, dscore, tailed = kept[span]
        query = query_ref[at, :]
        key = key_ref[at, :]
        key_wide = key.astype(F32)
        dright = mul_tn(inverse_ref[at, :], low(dfresh_ref[at, :]))
        dright_low = low(dright)
        dcouple = jnp.where(strict, -mul_nt(dright_low, fresh_ref[at, :]), 0.0)
        cross = mul_nt(key, key) * ratio
        weighted = dcouple * cross
        dbeta = jnp.sum(weighted, axis=1, keepdims=True)
        ratio_grad = dscore * score + weighted * beta
        dintersect = low(dcouple * beta * ratio)
        dscored = low(dscore * ratio)
        dquery = mul(dscored, key)
        dkey = mul_tn(dscored, query) + mul(dintersect, key) + mul_tn(dintersect, key)
        pieces = [[], [], []]
        for step in range(steps):
            index = span * steps + step
            here = slice(index * BLOCK, (index + 1) * BLOCK)
            joined = jnp.concatenate(
                [dout_ref[here, :], dright_low[step * BLOCK : (step + 1) * BLOCK]], axis=0
            )
            back = mul_nt(joined, state_ref[index])
            pieces[0].append(back[:BLOCK])
            pieces[1].append(back[BLOCK:])
            pieces[2].append(mul_nt(fresh_ref[here, :], dstate_ref[index]))
        out_back, right_back, tail_back = [jnp.concatenate(piece, axis=0) for piece in pieces]
        dquery = dquery + growth * out_back
        read = jnp.sum(key_wide * right_back, axis=1, keepdims=True)
        dkey = dkey - (beta * growth) * right_back + tail * tail_back
        dbeta = (
            dbeta
            + jnp.sum(dright * value_ref[at, :].astype(F32), axis=1, keepdims=True)
            - growth * read
        )
        dgrowth = jnp.sum(query.astype(F32) * out_back, axis=1, keepdims=True) - beta * read
        dtail = tail * jnp.sum(key_wide * tail_back, axis=1, keepdims=True)
        flat = jnp.sum(
            jnp.where(rows == cols, jnp.sum(ratio_grad, axis=0, keepdims=True), 0.0),
            axis=1,
            keepdims=True,
        )
        drunning = growth * dgrowth + jnp.sum(ratio_grad, axis=1, keepdims=True) - flat - dtail
        line = jnp.sum(jnp.where(rows == cols, drunning, 0.0), axis=0, keepdims=True)
        tail_line = jnp.sum(jnp.where(rows == cols, dtail, 0.0), axis=0, keepdims=True)
        ending = jnp.concatenate(
            [jnp.broadcast_to(ends[span * steps + step], (BLOCK, 1)) for step in range(steps)],
            axis=0,
        )
        dlog = (
            jnp.sum(jnp.where(same & (rows <= cols), line, 0.0), axis=1, keepdims=True)
            + jnp.sum(jnp.where(same, tail_line, 0.0), axis=1, keepdims=True)
            + ending
        )
        raw = raw_ref[at, :]
        ddecay = -jnp.exp(rate) * dlog * sigmoid(raw[:, 1:2] + bias)
        drate = drate + jnp.sum(dlog * column, axis=0, keepdims=True)
        dbias = dbias + jnp.sum(ddecay, axis=0, keepdims=True)
        dbeta = dbeta * beta * (1.0 - beta)
        lane = lax.broadcasted_iota(jnp.int32, (SPAN, 128), 1)
        draw = low(jnp.where(lane == 0, dbeta, jnp.where(lane == 1, ddecay, 0.0)))
        for half in range(SPAN // PART):
            held = part_rows(order_ref, span * (SPAN // PART) + half)
            dproj_ref[held, FRONT:WIDE] = draw[half * PART : (half + 1) * PART]
        dq_ref[at, :] = low(dquery)
        dk_ref[at, :] = low(dkey)
        dv_ref[at, :] = low(beta * dright)
    lane = lax.broadcasted_iota(jnp.int32, (8, 128), 1)
    drates_ref[...] = jnp.where(lane == 0, drate, jnp.where(lane == 1, dbias, 0.0))

    dtaps_ref[...] = jnp.zeros_like(dtaps_ref)
    halo_ref[...] = jnp.zeros_like(halo_ref)

    def back(step, carry):
        index = BLOCKS - 1 - step
        base = pl.multiple_of(index * BLOCK, BLOCK)
        held = held_rows(order_ref, index)
        before = past_rows(order_ref, index)
        broken = (base == 0) | (base == start)
        ended = (base + BLOCK == TOTAL) | (base + BLOCK == start)
        for at in range(0, FRONT, DK):
            here = slice(at, at + DK)
            taps = taps_ref[:, here]
            halo = jnp.where(broken, 0.0, proj_ref[pl.ds(before, 8), here])
            block = proj_ref[pl.ds(held, BLOCK), here]
            joined = jnp.concatenate([halo, block], axis=0)
            shifted = [block] + [pltpu.roll(joined, offset, 0)[8:] for offset in range(1, 4)]
            conv = shifted[0] * taps[0:1]
            for offset in range(1, 4):
                conv = conv + shifted[offset] * taps[offset : offset + 1]
            sig = sigmoid(conv)
            if at >= 2 * DK:
                dact = dv_ref[pl.ds(base, BLOCK), at - 2 * DK : at - DK].astype(F32)
            else:
                act = conv * sig
                given = (dq_ref if at == 0 else dk_ref)[pl.ds(base, BLOCK), :].astype(F32)
                inv = lax.rsqrt(jnp.sum(act * act, axis=1, keepdims=True) + 1e-06)
                along = jnp.sum(act * given, axis=1, keepdims=True)
                dact = inv * (given - act * (inv * inv * along))
                if at == 0:
                    dact = dact * DK ** (-0.5)
            dconv = dact * (sig * (1.0 + conv * (1.0 - sig)))
            after = jnp.where(ended, 0.0, halo_ref[:, here])
            halo_ref[:, here] = dconv[:8]
            trailing = jnp.concatenate([dconv, after], axis=0)
            dblock = dconv * taps[0:1]
            for offset in range(1, 4):
                moved = pltpu.roll(trailing, BLOCK + 8 - offset, 0)[:BLOCK]
                dblock = dblock + moved * taps[offset : offset + 1]
            dproj_ref[pl.ds(held, BLOCK), here] = low(dblock)
            for offset in range(4):
                dtaps_ref[offset : offset + 1, here] += jnp.sum(
                    dconv * shifted[offset], axis=0, keepdims=True
                )
        return carry

    lax.fori_loop(0, BLOCKS, back, 0)


def run_kernel(kernel, name, scalars, arrays, results, scratch, cost):
    return pl.pallas_call(
        kernel,
        out_shape=tuple(jax.ShapeDtypeStruct(shape, kind) for shape, kind in results),
        in_specs=[pl.BlockSpec(memory_space=SMEM)] * len(scalars)
        + [pl.BlockSpec(memory_space=VMEM)] * len(arrays),
        out_specs=tuple([pl.BlockSpec(memory_space=VMEM)] * len(results)),
        scratch_shapes=[pltpu.VMEM(shape, kind) for shape, kind in scratch],
        compiler_params=pltpu.CompilerParams(vmem_limit_bytes=LIMIT),
        cost_estimate=pl.CostEstimate(
            flops=cost * 1_000_000_000, bytes_accessed=8_000_000, transcendentals=1_000_000
        ),
        name=name,
    )(*scalars, *arrays)


def front_call(lengths, order, rates, proj, taps):
    results = (
        ((TOTAL, DK), BF16),
        ((TOTAL, DK), BF16),
        ((TOTAL, DV), BF16),
        ((TOTAL, 128), F32),
        ((TOTAL, SPAN), BF16),
        ((TOTAL, DK), BF16),
        ((TOTAL, DV), F32),
        ((TOTAL, DK), BF16),
        ((TOTAL, SPAN), BF16),
        ((TOTAL, 128), F32),
    )
    return run_kernel(
        front_kernel, "mixer_front", (lengths, order, rates), (proj, taps), results, (), 12
    )


def chain_call(lengths, order, query, reach, base, tail, score, growth, gate, gain):
    results = (
        ((TOTAL, DV), BF16),
        ((BLOCKS, DK, DV), BF16),
        ((TOTAL, DV), BF16),
        ((TOTAL, DV), F32),
    )
    return run_kernel(
        chain_kernel,
        "mixer_chain",
        (lengths, order),
        (query, reach, base, tail, score, growth, gate, gain),
        results,
        (((DK, DV), F32),),
        12,
    )


def gate_back_call(lengths, order, grad, gate, gain, out):
    results = (((TOTAL, DV), BF16), ((TOTAL, DV), BF16), ((1, DV), F32))
    return run_kernel(
        gate_back_kernel, "gate_back", (lengths, order), (grad, gate, gain, out), results, (), 4
    )


def back_call(lengths, order, rates, arrays):
    results = (((TOTAL, WIDE), BF16), ((4, FRONT), F32), ((8, 128), F32))
    scratch = (
        ((TOTAL, DV), F32),
        ((BLOCKS, DK, DV), BF16),
        ((DK, DV), F32),
        ((TOTAL, DK), BF16),
        ((TOTAL, DK), BF16),
        ((TOTAL, DV), BF16),
        ((8, FRONT), F32),
    )
    return run_kernel(
        back_kernel, "mixer_back", (lengths, order, rates), arrays, results, scratch, 50
    )


def plain_product(left, right):
    return jnp.dot(left, right, preferred_element_type=F32)


def transposed_product(left, right):
    return lax.dot_general(left, right, (((0,), (0,)), ((), ())), preferred_element_type=F32)


def product_back(grad, weight):
    return lax.dot_general(grad, weight, (((1,), (1,)), ((), ())), preferred_element_type=F32)


def plain_scale(value, gain):
    return value * lax.rsqrt(jnp.mean(value * value, axis=-1, keepdims=True) + 1e-06) * gain


class Ring:
    def __init__(self, count):
        self.count = count
        self.circle = count % 2 == 0 and 4 <= count <= 16
        if self.circle:
            self.order = list(range(0, count, 2)) + list(range(count - 1, 0, -2))
        else:
            self.order = list(range(count))
        place = [self.order.index(i) for i in range(count)]
        here = lax.axis_index("dp")
        if self.circle:
            ahead = [[self.order[(place[i] + d) % count] for d in range(count)] for i in range(count)]
            behind = [[(place[j] - place[i]) % count for j in range(count)] for i in range(count)]
            self.ahead = jnp.array(ahead, jnp.int32)[here]
            self.behind = jnp.array(behind, jnp.int32)[here]

    def step(self, value, forward):
        pairs = [(self.order[i], self.order[(i + 1) % self.count]) for i in range(self.count)]
        if not forward:
            pairs = [(b, a) for a, b in pairs]
        return lax.ppermute(value, "dp", pairs)

    def gather(self, parts):
        if not self.circle:
            whole = [lax.all_gather(part, "dp", axis=0) for part in parts]
            return [[one[d] for d in range(self.count)] for one in whole]
        middle = self.count // 2
        result = []
        for part in parts:
            pieces = [None] * self.count
            pieces[0] = part
            up = down = part
            for hop in range(1, middle):
                up = self.step(up, True)
                down = self.step(down, False)
                pieces[self.count - hop] = up
                pieces[hop] = down
            cut = part.shape[0] // 2
            pieces[middle] = jnp.concatenate(
                [self.step(up[:cut], True), self.step(down[cut:], False)], axis=0
            )
            result.append(pieces)
        return result

    def scatter_sum(self, pieces):
        kind = pieces[0].dtype
        if not self.circle:
            whole = jnp.stack(pieces)
            return lax.psum_scatter(whole, "dp", scatter_dimension=0, tiled=False).astype(F32)
        middle = self.count // 2
        cut = pieces[0].shape[0] // 2
        up = self.step(pieces[middle][:cut], True).astype(F32)
        down = self.step(pieces[middle][cut:], False).astype(F32)
        for hop in range(middle - 1, 0, -1):
            ahead = pieces[hop].astype(F32)
            back = pieces[self.count - hop].astype(F32)
            if hop == middle - 1:
                ahead = jnp.concatenate([ahead[:cut] + up, ahead[cut:]], axis=0)
                back = jnp.concatenate([back[:cut], back[cut:] + down], axis=0)
            else:
                ahead = ahead + up
                back = back + down
            up = self.step(ahead.astype(kind), True).astype(F32)
            down = self.step(back.astype(kind), False).astype(F32)
        return pieces[0].astype(F32) + up + down

    def to_ahead(self, value):
        return self.reorder(value, "ahead")

    def to_mesh(self, value):
        return self.reorder(value, "behind")

    def reorder(self, value, which):
        if not self.circle:
            return value
        index = getattr(self, which)
        width = value.shape[1] // self.count
        return jnp.concatenate(
            [
                lax.dynamic_slice_in_dim(value, index[d] * width, width, axis=1)
                for d in range(self.count)
            ],
            axis=1,
        )


def swap(value, distance):
    count = lax.axis_size("tensor")
    return lax.ppermute(value, "tensor", [(i, i ^ distance) for i in range(count)])


def team_gather(value):
    other = swap(value, 2)
    near = swap(value, 1)
    far = swap(other, 1)
    return jnp.concatenate([value, other, near, far], axis=0)


def team_sum_rows(value):
    half = value.shape[0] // 2
    got = swap(value[half:], 1)
    both = value[:half].astype(F32) + got.astype(F32)
    quarter = half // 2
    return both[:quarter] + swap(low(both[quarter:]), 2).astype(F32)


def team_sum(value):
    value = value + swap(value, 1)
    return value + swap(value, 2)


def local(
    tokens,
    lengths,
    cotangent,
    norm_gain,
    query_weight,
    key_weight,
    value_weight,
    gate_weight,
    beta_weight,
    decay_weight,
    query_conv,
    key_conv,
    value_conv,
    decay_params,
    head_gain,
    out_weight,
    ffn_gain,
    ffn_gate,
    ffn_up,
    ffn_down,
):
    count = lax.axis_size("dp")
    team = lax.axis_size("tensor")
    ring = Ring(count)
    place = lax.axis_index("tensor")
    swapped = [[[0, 2, 1, 3][i ^ t] for i in range(team)] for t in range(team)]
    order = jnp.array(swapped, jnp.int32)[place]
    share = norm_gain.shape[0]
    narrow = head_gain.shape[0]

    channels = jnp.concatenate([query_conv, key_conv, value_conv], axis=1)
    pack = jnp.concatenate(
        [
            beta_weight,
            decay_weight,
            norm_gain[:, None],
            ffn_gain[:, None],
            channels.T,
            jnp.pad(head_gain, (0, share - narrow))[:, None],
            jnp.zeros((share, 119), BF16),
        ],
        axis=1,
    )
    entry = jnp.concatenate([query_weight, key_weight, value_weight, pack], axis=1)
    rows_here = tokens.shape[0]
    tokens = ring.to_ahead(tokens)
    cotangent = ring.to_ahead(cotangent)
    both_whole = team_gather(jnp.concatenate([tokens, cotangent], axis=1))
    width = tokens.shape[1]
    tokens_whole = both_whole[:, :width]
    down_grad = both_whole[:, width:]

    (entry_pieces,) = ring.gather([entry])
    entry_whole = jnp.concatenate(entry_pieces, axis=0)
    gate_pieces, out_pieces = ring.gather([gate_weight, out_weight])
    gate_whole = jnp.concatenate(gate_pieces, axis=0)
    out_whole = jnp.concatenate(out_pieces, axis=1)
    wide_pieces, down_pieces = ring.gather(
        [jnp.concatenate([ffn_gate, ffn_up], axis=1), ffn_down]
    )
    wide_whole = jnp.concatenate(wide_pieces, axis=0)
    down_whole = jnp.concatenate(down_pieces, axis=1)

    pack_whole = entry_whole[:, FRONT:WIDE]
    norm_whole = pack_whole[:, 2].astype(F32)
    ffn_gain_whole = pack_whole[:, 3].astype(F32)
    small = pack_whole[:, 4:9].astype(F32).reshape(count, share, 5)
    if ring.circle:
        small = small[ring.behind]
    narrow_q = query_conv.shape[1]
    cuts = (0, narrow_q, 2 * narrow_q, share)
    taps = jnp.concatenate(
        [small[:, a:b, :4].reshape(-1, 4) for a, b in zip(cuts[:-1], cuts[1:])], axis=0
    ).T
    gains = small[:, :narrow, 4].reshape(1, DV)

    token_rows = tokens.astype(F32)
    all_rows = tokens_whole.astype(F32)
    unit_rows = all_rows * lax.rsqrt(jnp.mean(all_rows * all_rows, axis=-1, keepdims=True) + 1e-06)
    mixer_input = (unit_rows * norm_whole).astype(BF16)
    proj = plain_product(mixer_input, entry_whole)
    (
        query,
        key,
        value,
        raw,
        inverse,
        reach,
        base,
        tail,
        score,
        growth,
    ) = front_call(lengths, order, decay_params, proj, taps)
    gate_proj = plain_product(mixer_input, gate_whole)
    gated, state, fresh, out = chain_call(
        lengths, order, query, reach, base, tail, score, growth, gate_proj, gains
    )
    mixed = team_sum_rows(plain_product(gated, out_whole).astype(BF16))
    middle = token_rows + mixed
    second_norm, second_pull = jax.vjp(plain_scale, middle, ffn_gain_whole)
    ffn_input = team_gather(second_norm.astype(BF16))
    hidden = wide_whole.shape[1] // 2
    acts = plain_product(ffn_input, wide_whole)
    gate_act = acts[:, :hidden]
    up_act = acts[:, hidden:]
    sigmoid_gate = jax.nn.sigmoid(gate_act)
    swish = gate_act * sigmoid_gate
    product_rows = (swish * up_act).astype(BF16)
    ffn_out = team_sum_rows(plain_product(product_rows, down_whole).astype(BF16))
    block_out = ring.to_mesh((middle + ffn_out).astype(BF16))

    grad_product = product_back(down_grad, down_whole)
    grad_gate_act = (
        grad_product * up_act * sigmoid_gate * (1.0 + gate_act * (1.0 - sigmoid_gate))
    ).astype(BF16)
    grad_up_act = (grad_product * swish).astype(BF16)
    grad_acts = jnp.concatenate([grad_gate_act, grad_up_act], axis=1)
    ffn_input_part = product_back(grad_acts, wide_whole)
    grad_second = team_sum_rows(ffn_input_part.astype(BF16))
    grad_middle_norm, grad_ffn_gain = second_pull(grad_second)
    grad_middle = cotangent.astype(F32) + grad_middle_norm
    grad_mixed = team_gather(grad_middle.astype(BF16))

    grad_wide = transposed_product(ffn_input, grad_acts).astype(BF16)
    grad_down = transposed_product(product_rows, down_grad).astype(BF16)

    def by_rows(value):
        return [value[d * share : (d + 1) * share] for d in range(count)]

    def by_cols(value):
        return [value[:, d * share : (d + 1) * share] for d in range(count)]

    wide_sum = ring.scatter_sum(by_rows(grad_wide))
    down_sum = ring.scatter_sum(by_cols(grad_down))

    grad_out = transposed_product(gated, grad_mixed).astype(BF16)
    out_sum = ring.scatter_sum(by_cols(grad_out))
    grad_gated = product_back(grad_mixed, out_whole)
    dgate, dout, dgain = gate_back_call(lengths, order, grad_gated, gate_proj, gains, out)
    grad_gate = transposed_product(mixer_input, dgate).astype(BF16)
    gate_sum = ring.scatter_sum(by_rows(grad_gate))
    dproj, dtaps, drates = back_call(
        lengths,
        order,
        decay_params,
        (proj, taps, dout, raw, query, key, value, state, inverse, reach, fresh),
    )
    grad_entry = transposed_product(mixer_input, dproj)
    entry_sum = ring.scatter_sum(by_rows(low(grad_entry[:, :FRONT])))
    input_part = product_back(dproj, entry_whole) + product_back(dgate, gate_whole)
    grad_first = team_sum_rows(input_part.astype(BF16))
    first_unit = lax.rsqrt(jnp.mean(token_rows * token_rows, axis=-1, keepdims=True) + 1e-06)
    pulled = grad_first * norm_whole
    grad_tokens_norm = first_unit * pulled - token_rows * (
        first_unit * first_unit * first_unit * jnp.mean(pulled * token_rows, axis=-1, keepdims=True)
    )
    tokens_grad = ring.to_mesh(grad_middle + grad_tokens_norm)
    grad_norm_gain = jnp.sum(input_part * unit_rows, axis=0)

    gain_sums = team_sum(jnp.stack([grad_norm_gain, grad_ffn_gain], axis=1))
    channel_parts = [
        dtaps[:, a * count : b * count].T.reshape(count, b - a, 4)
        for a, b in zip(cuts[:-1], cuts[1:])
    ]
    channel_grads = jnp.concatenate(
        [
            jnp.concatenate(channel_parts, axis=1),
            jnp.pad(dgain.reshape(count, narrow, 1), ((0, 0), (0, share - narrow), (0, 0))),
        ],
        axis=2,
    )
    if ring.circle:
        channel_grads = channel_grads[ring.ahead]
    pack_grad = jnp.concatenate(
        [
            grad_entry[:, FRONT : FRONT + 2],
            gain_sums,
            channel_grads.reshape(count * share, 5),
            jnp.broadcast_to(drates[0:1, 0:2], (count * share, 2)),
            jnp.zeros((count * share, 117), F32),
        ],
        axis=1,
    )
    pack_sum = ring.scatter_sum(by_rows(pack_grad))
    tap_sum = pack_sum[:, 4:8].T
    return (
        block_out,
        tokens_grad,
        pack_sum[:, 2],
        entry_sum[:, :DK],
        entry_sum[:, DK : 2 * DK],
        entry_sum[:, 2 * DK :],
        gate_sum,
        pack_sum[:, 0:1],
        pack_sum[:, 1:2],
        tap_sum[:, cuts[0] : cuts[1]],
        tap_sum[:, cuts[1] : cuts[2]],
        tap_sum[:, cuts[2] : cuts[3]],
        pack_sum[0, 9:11][:, None],
        pack_sum[:narrow, 8],
        out_sum,
        pack_sum[:, 3],
        wide_sum[:, :hidden],
        wide_sum[:, hidden:],
        down_sum,
    )


def solution(mesh):
    rows = P(("dp", "tensor"), None)
    weight = P("dp", "tensor")
    channel = P(None, ("tensor", "dp"))
    down = P("tensor", "dp")
    return jax.shard_map(
        local,
        mesh=mesh,
        in_specs=(
            rows,
            P("dp", None),
            rows,
            P("dp"),
            weight,
            weight,
            weight,
            weight,
            weight,
            weight,
            channel,
            channel,
            channel,
            P(None, "tensor"),
            P(("tensor", "dp")),
            down,
            P("dp"),
            weight,
            weight,
            down,
        ),
        out_specs=(
            rows,
            rows,
            P("dp"),
            weight,
            weight,
            weight,
            weight,
            weight,
            weight,
            channel,
            channel,
            channel,
            P(None, "tensor"),
            P(("tensor", "dp")),
            down,
            P("dp"),
            weight,
            weight,
            down,
        ),
        check_vma=False,
    )
```

```python
import jax
import jax.numpy as jnp
from jax import lax
from jax.experimental import pallas as pl
from jax.experimental.pallas import tpu as pltpu
from jax.sharding import PartitionSpec as P

DK = 256
DV = 512
BLOCK = 64
SPAN = 256
PART = 128
TOTAL = 512
FRONT = 2 * DK + DV
PACK = 16
PIECES = 8
MIDDLE = PIECES // 2
BLOCKS = TOTAL // BLOCK
SPANS = TOTAL // SPAN
F32 = jnp.float32
BF16 = jnp.bfloat16
SMEM = pltpu.SMEM
VMEM = pltpu.VMEM
LIMIT = 56 * 1024 * 1024


def mul(left, right):
    return lax.dot_general(left, right, (((1,), (0,)), ((), ())), preferred_element_type=F32)


def mul_nt(left, right):
    return lax.dot_general(left, right, (((1,), (1,)), ((), ())), preferred_element_type=F32)


def mul_tn(left, right):
    return lax.dot_general(left, right, (((0,), (0,)), ((), ())), preferred_element_type=F32)


def low(value):
    return value.astype(BF16)


def halves(value):
    high = low(value)
    return high, low(value - high.astype(F32))


def fine(product, left, right):
    return product(left[0], right[0]) + (product(left[0], right[1]) + product(left[1], right[0]))


def mul_fine(left, right):
    return fine(mul, halves(left), halves(right))


def keep_halves(ref, at, pair):
    width = pair[0].shape[1]
    ref[at, :width] = pair[0]
    ref[at, width:] = pair[1]


def read_halves(ref, at):
    width = ref.shape[1] // 2
    return ref[at, :width], ref[at, width:]


def rows_of(*values):
    return jnp.concatenate(values, axis=0)


def sigmoid(value):
    return 1.0 / (1.0 + jnp.exp(-value))


def softplus(value):
    return jnp.maximum(value, 0.0) + jnp.log1p(jnp.exp(-jnp.abs(value)))


def span_masks():
    rows = lax.broadcasted_iota(jnp.int32, (SPAN, SPAN), 0)
    cols = lax.broadcasted_iota(jnp.int32, (SPAN, SPAN), 1)
    same = (rows // BLOCK) == (cols // BLOCK)
    return rows, cols, same


def decay_terms(raw, rate, bias, masks):
    rows, cols, same = masks
    causal = same & (rows >= cols)
    column = -jnp.exp(rate) * softplus(raw + bias)
    line = jnp.sum(jnp.where(rows == cols, column, 0.0), axis=0, keepdims=True)
    running = jnp.sum(jnp.where(causal, line, 0.0), axis=1, keepdims=True)
    running_line = jnp.sum(jnp.where(same & (rows <= cols), column, 0.0), axis=0, keepdims=True)
    final = jnp.sum(jnp.where(same, line, 0.0), axis=1, keepdims=True)
    ratio = jnp.where(causal, jnp.exp(jnp.where(causal, running - running_line, 0.0)), 0.0)
    return column, running, final, ratio


def unit_inverse(coupling, masks):
    rows, cols, same = masks
    inverse = jnp.where(rows == cols, 1.0, 0.0) - jnp.where(
        (rows // 2 == cols // 2), coupling, 0.0
    )
    width = 2
    while width < BLOCK:
        inner = (rows // (2 * width) == cols // (2 * width)) & (rows // width != cols // width)
        part = jnp.where(inner, coupling, 0.0)
        inverse = inverse - mul_fine(mul_fine(inverse, part), inverse)
        width = width * 2
    return inverse


def second_start(lengths_ref):
    return (lengths_ref[0, 0] + BLOCK - 1) // BLOCK * BLOCK


def held_rows(order_ref, index):
    half = index % 2
    return pl.multiple_of(order_ref[index // 2] * PART + half * BLOCK, BLOCK)


def part_rows(order_ref, index):
    return pl.ds(pl.multiple_of(order_ref[index] * PART, PART), PART)


def past_rows(order_ref, index):
    return pl.multiple_of(held_rows(order_ref, jnp.maximum(index - 1, 0)) + BLOCK - 8, 8)


def row_limit(lengths_ref, start, base, count):
    place = lax.broadcasted_iota(jnp.int32, (count, 1), 0) + base
    limit = jnp.where(place >= start, start + lengths_ref[0, 1], lengths_ref[0, 0])
    return place < limit


def fill_weight(pieces, weight_ref, cols):
    at = 0
    total = weight_ref.shape[0]
    middle = (len(pieces) - 1) // 2
    share = total // (len(pieces) - 1)
    for index, piece in enumerate(pieces):
        count = share // 2 if index in (middle, middle + 1) else share
        weight_ref[at : at + count, :] = piece[:count, cols]
        at += count


def norm_of(rows, gain):
    return low(rows * lax.rsqrt(jnp.mean(rows * rows, axis=1, keepdims=True) + 1e-06) * gain)


def ahead_copy(ahead_ref, source_ref, target_ref, rows):
    count = ahead_ref.shape[0]
    share = target_ref.shape[1] // count
    for d in range(count):
        cols = pl.ds(pl.multiple_of(ahead_ref[d] * share, share), share)
        target_ref[rows, d * share : (d + 1) * share] = source_ref[:, cols]


def gather_kernel(ahead_ref, norm_ref, *refs):
    input_ref, grad_ref, wide_ref = refs[-3:]
    size = wide_ref.shape[0]
    for at in range(4):
        rows = slice(at * size, (at + 1) * size)
        ahead_copy(ahead_ref, refs[at], wide_ref, slice(None))
        ahead_copy(ahead_ref, refs[4 + at], grad_ref, rows)
        input_ref[rows, :] = norm_of(wide_ref[...].astype(F32), norm_ref[...])


def front_kernel(
    lengths_ref,
    order_ref,
    rates_ref,
    taps_ref,
    input_ref,
    small_ref,
    *refs,
):
    pieces = refs[:-12]
    (
        proj_ref,
        query_ref,
        key_ref,
        value_ref,
        raw_ref,
        inverse_ref,
        reach_ref,
        base_ref,
        tail_ref,
        score_ref,
        growth_ref,
        weight_ref,
    ) = refs[-12:]
    fill_weight(pieces, weight_ref, slice(0, FRONT))
    for half in range(TOTAL // SPAN):
        rows = slice(half * SPAN, (half + 1) * SPAN)
        proj_ref[rows, :] = mul(input_ref[rows, :], weight_ref[...])
    start = second_start(lengths_ref)
    rate = rates_ref[0, 0]
    bias = rates_ref[1, 0]

    def front(index, carry):
        base = pl.multiple_of(index * BLOCK, BLOCK)
        held = held_rows(order_ref, index)
        before = past_rows(order_ref, index)
        broken = (base == 0) | (base == start)
        for at in range(0, FRONT, DK):
            here = slice(at, at + DK)
            taps = taps_ref[:, here]
            halo = jnp.where(broken, 0.0, proj_ref[pl.ds(before, 8), here])
            block = proj_ref[pl.ds(held, BLOCK), here]
            joined = jnp.concatenate([halo, block], axis=0)
            conv = block * taps[0:1]
            for offset in range(1, 4):
                conv = conv + pltpu.roll(joined, offset, 0)[8:] * taps[offset : offset + 1]
            act = conv * sigmoid(conv)
            if at >= 2 * DK:
                value_ref[pl.ds(base, BLOCK), at - 2 * DK : at - DK] = low(act)
            else:
                inv = lax.rsqrt(jnp.sum(act * act, axis=1, keepdims=True) + 1e-06)
                if at == 0:
                    query_ref[pl.ds(base, BLOCK), :] = low(act * inv * DK ** (-0.5))
                else:
                    key_ref[pl.ds(base, BLOCK), :] = low(act * inv)
        return carry

    lax.fori_loop(0, BLOCKS, front, 0)
    for part in range(TOTAL // PART):
        raw_ref[part * PART : (part + 1) * PART, :] = mul_nt(
            input_ref[part_rows(order_ref, part), :], small_ref[...]
        )

    masks = span_masks()
    rows, cols, same = masks
    strict = same & (rows > cols)
    lane = lax.broadcasted_iota(jnp.int32, (SPAN, 128), 1)
    for span in range(SPANS):
        at = slice(span * SPAN, (span + 1) * SPAN)
        raw = raw_ref[at, :]
        beta = sigmoid(raw[:, 0:1])
        _, running, final, ratio = decay_terms(raw[:, 1:2], rate, bias, masks)
        growth = jnp.exp(running)
        key = key_ref[at, :]
        coupling = jnp.where(strict, beta * mul_nt(key, key) * ratio, 0.0)
        inverse = halves(unit_inverse(coupling, masks))
        keep_halves(inverse_ref, at, inverse)
        key_wide = key.astype(F32)
        base_ref[at, :] = fine(mul, inverse, halves(beta * value_ref[at, :].astype(F32)))
        reach = fine(mul, inverse, halves(beta * growth * key_wide))
        keep_halves(reach_ref, at, halves(reach))
        keep_halves(tail_ref, at, halves(jnp.exp(final - running) * key_wide))
        keep_halves(score_ref, at, halves(mul_nt(query_ref[at, :], key) * ratio))
        growth_ref[at, :] = jnp.where(lane == 0, growth, jnp.exp(final))


def chain_kernel(
    lengths_ref,
    query_ref,
    reach_ref,
    base_ref,
    tail_ref,
    score_ref,
    growth_ref,
    state_ref,
    fresh_ref,
    out_ref,
    carry_ref,
):
    start = second_start(lengths_ref)
    carry_ref[...] = jnp.zeros_like(carry_ref)
    for index in range(BLOCKS):
        at = slice(index * BLOCK, (index + 1) * BLOCK)
        held = jnp.where(start == index * BLOCK, 0.0, carry_ref[...])
        state = low(held)
        state_ref[index] = state
        both = mul(rows_of(*read_halves(reach_ref, at), query_ref[at, :]), state)
        fresh = halves(base_ref[at, :] - both[:BLOCK] - both[BLOCK : 2 * BLOCK])
        keep_halves(fresh_ref, at, fresh)
        out_ref[at, :] = growth_ref[at, 0:1] * both[2 * BLOCK :]
        if index + 1 < BLOCKS:
            final = growth_ref[index * BLOCK : index * BLOCK + 1, 1:2]
            tail = read_halves(tail_ref, at)
            carry_ref[...] = final * held + mul_tn(
                rows_of(*tail, tail[0]), rows_of(fresh[0], fresh[0], fresh[1])
            )

    for part in range(TOTAL // PART):
        span = part * PART // SPAN
        here = slice(part * PART, (part + 1) * PART)
        fresh = read_halves(fresh_ref, slice(span * SPAN, (span + 1) * SPAN))
        out = out_ref[here, :] + fine(mul, read_halves(score_ref, here), fresh)
        out_ref[here, :] = jnp.where(row_limit(lengths_ref, start, part * PART, PART), out, 0.0)


def gate_kernel(order_ref, out_ref, gain_ref, input_ref, *refs):
    pieces = refs[:-5]
    gate_ref, gated_ref, keep_ref, send_ref, weight_ref = refs[-5:]
    fill_weight(pieces, weight_ref, slice(0, 2 * DV))
    for half in range(TOTAL // SPAN):
        rows = slice(half * SPAN, (half + 1) * SPAN)
        gate_ref[rows, :] = mul(input_ref[rows, :], weight_ref[:, :DV])
    gain = gain_ref[...]
    for part in range(TOTAL // PART):
        out = out_ref[part * PART : (part + 1) * PART, :]
        inv = lax.rsqrt(jnp.mean(out * out, axis=1, keepdims=True) + 1e-06)
        held = part_rows(order_ref, part)
        gate = gate_ref[held, :]
        gated_ref[held, :] = low(out * inv * gain * (gate * sigmoid(gate)))
    for half, mixed_ref in enumerate((keep_ref, send_ref)):
        rows = slice(half * SPAN, (half + 1) * SPAN)
        mixed_ref[...] = low(mul_nt(gated_ref[rows, :], weight_ref[:, DV:]))


def write_grads(pieces, pairs):
    count = len(pieces) - 1
    middle = count // 2
    total = pairs[0][0].shape[1]
    share = total // count
    for block in range(total // SPAN):
        here = slice(block * SPAN, (block + 1) * SPAN)
        at = 0
        for left_ref, right_ref in pairs:
            width = right_ref.shape[1]
            part = low(mul_tn(left_ref[:, here], right_ref[...]))
            for step in range(SPAN // share):
                d = block * (SPAN // share) + step
                rows = part[step * share : (step + 1) * share]
                if d == middle and pieces[d] is None:
                    continue
                if d == middle:
                    pieces[d][:, at : at + width] = rows[: share // 2]
                    pieces[d + 1][:, at : at + width] = rows[share // 2 :]
                else:
                    pieces[d + (d > middle)][:, at : at + width] = rows
            at += width
    for piece in pieces:
        if piece is not None and at < piece.shape[1]:
            piece[:, at:] = jnp.zeros((piece.shape[0], piece.shape[1] - at), BF16)


def ffn_kernel(grad_ref, first_ref, second_ref, third_ref, fourth_ref, *refs):
    pieces = refs[:-10]
    (
        input_ref,
        out_keep_ref,
        out_send_ref,
        back_keep_ref,
        back_send_ref,
        product_ref,
        grads_ref,
        up_ref,
        down_ref,
        weight_ref,
    ) = refs[-10:]
    hidden = product_ref.shape[1]
    own = first_ref.shape[0]
    for at, part in enumerate((first_ref, second_ref, third_ref, fourth_ref)):
        input_ref[at * own : (at + 1) * own, :] = part[...]
    fill_weight(pieces, weight_ref, slice(0, 3 * hidden))
    for half in range(TOTAL // SPAN):
        rows = slice(half * SPAN, (half + 1) * SPAN)
        acts = mul(input_ref[rows, :], weight_ref[:, : 2 * hidden])
        gate = acts[:, :hidden]
        up = acts[:, hidden:]
        sig = sigmoid(gate)
        swish = gate * sig
        product = low(swish * up)
        product_ref[rows, :] = product
        down = weight_ref[:, 2 * hidden :]
        (out_keep_ref, out_send_ref)[half][...] = low(mul_nt(product, down))
        dproduct = mul(grad_ref[rows, :], down)
        dgate = dproduct * up * sig * (1.0 + gate * (1.0 - sig))
        grads_ref[rows, :] = low(jnp.concatenate([dgate, dproduct * swish], axis=1))
        (back_keep_ref, back_send_ref)[half][...] = low(
            mul_nt(grads_ref[rows, :], weight_ref[:, : 2 * hidden])
        )
    width = input_ref.shape[1]
    here = slice(width // 2, width // 2 + width // PIECES)
    cut = up_ref.shape[0]
    at = 0
    for left_ref, right_ref in ((input_ref, grads_ref), (grad_ref, product_ref)):
        cols = slice(at, at + right_ref.shape[1])
        part = low(mul_tn(left_ref[:, here], right_ref[...]))
        up_ref[:, cols] = part[:cut]
        down_ref[:, cols] = part[cut:]
        at += right_ref.shape[1]
    for half_ref in (up_ref, down_ref):
        half_ref[:, at:] = jnp.zeros((cut, half_ref.shape[1] - at), BF16)


def ffn_grads_kernel(input_ref, grads_ref, outer_ref, product_ref, *pieces):
    pieces = [*pieces[:MIDDLE], None, None, *pieces[MIDDLE:]]
    write_grads(pieces, [(input_ref, grads_ref), (outer_ref, product_ref)])


def entry_grads_kernel(input_ref, grads_ref, *pieces):
    write_grads(pieces, [(input_ref, grads_ref)])


def input_back_kernel(
    ahead_ref,
    dproj_ref,
    dgate_ref,
    draw_ref,
    small_ref,
    first_ref,
    second_ref,
    third_ref,
    fourth_ref,
    *refs,
):
    count = (len(refs) - 6) // 2
    keep_ref, send_ref, gain_ref, wide_ref, entry_ref, gate_ref = refs[2 * count :]
    fill_weight(refs[:count], entry_ref, slice(0, FRONT))
    fill_weight(refs[count : 2 * count], gate_ref, slice(0, DV))
    size = wide_ref.shape[0]
    gain = jnp.zeros(gain_ref.shape, F32)
    tokens = (first_ref, second_ref, third_ref, fourth_ref)
    for half, out_ref in enumerate((keep_ref, send_ref)):
        rows = slice(half * SPAN, (half + 1) * SPAN)
        back = mul_nt(dproj_ref[rows, :], entry_ref[...]) + mul_nt(dgate_ref[rows, :], gate_ref[...])
        back = back + mul(draw_ref[rows, :], small_ref[...])
        out_ref[...] = low(back)
        for step in range(SPAN // size):
            ahead_copy(ahead_ref, tokens[half * (SPAN // size) + step], wide_ref, slice(None))
            token = wide_ref[...].astype(F32)
            inv = lax.rsqrt(jnp.mean(token * token, axis=1, keepdims=True) + 1e-06)
            grad = back[step * size : (step + 1) * size]
            gain = gain + jnp.sum(grad * token * inv, axis=0, keepdims=True)
    gain_ref[...] = gain


def summed(keep_ref, near_ref, far_ref):
    own = far_ref.shape[0]
    total = keep_ref[:own, :].astype(F32) + near_ref[:own, :].astype(F32)
    return total + far_ref[...].astype(F32)


def middle_kernel(ahead_ref, tokens_ref, keep_ref, near_ref, far_ref, gain_ref, middle_ref, input_ref, wide_ref):
    ahead_copy(ahead_ref, tokens_ref, wide_ref, slice(None))
    middle = wide_ref[...].astype(F32) + summed(keep_ref, near_ref, far_ref)
    middle_ref[...] = middle
    input_ref[...] = norm_of(middle, gain_ref[...])


def norm_back(rows, grad, gain):
    inv = lax.rsqrt(jnp.mean(rows * rows, axis=1, keepdims=True) + 1e-06)
    pulled = grad * gain
    back = inv * pulled - rows * (inv * inv * inv * jnp.mean(pulled * rows, axis=1, keepdims=True))
    return back, jnp.sum(grad * rows * inv, axis=0, keepdims=True)


def middle_back_kernel(
    ahead_ref, cotangent_ref, middle_ref, keep_ref, near_ref, far_ref, gain_ref, back_ref, low_ref, dgain_ref, wide_ref
):
    ahead_copy(ahead_ref, cotangent_ref, wide_ref, slice(None))
    grad = summed(keep_ref, near_ref, far_ref)
    back, dgain = norm_back(middle_ref[...], grad, gain_ref[...])
    back = wide_ref[...].astype(F32) + back
    back_ref[...] = back
    low_ref[...] = low(back)
    dgain_ref[...] = dgain


def mesh_copy(ahead_ref, source, target_ref):
    count = ahead_ref.shape[0]
    share = target_ref.shape[1] // count
    for d in range(count):
        cols = pl.ds(pl.multiple_of(ahead_ref[d] * share, share), share)
        target_ref[:, cols] = source[:, d * share : (d + 1) * share]


def tokens_back_kernel(ahead_ref, tokens_ref, middle_ref, keep_ref, near_ref, far_ref, gain_ref, out_ref, wide_ref):
    ahead_copy(ahead_ref, tokens_ref, wide_ref, slice(None))
    grad = summed(keep_ref, near_ref, far_ref)
    back, _ = norm_back(wide_ref[...].astype(F32), grad, gain_ref[...])
    mesh_copy(ahead_ref, middle_ref[...] + back, out_ref)


def block_out_kernel(ahead_ref, middle_ref, keep_ref, near_ref, far_ref, out_ref):
    mesh_copy(ahead_ref, low(middle_ref[...] + summed(keep_ref, near_ref, far_ref)), out_ref)


def gate_back_kernel(
    lengths_ref,
    order_ref,
    first_ref,
    second_ref,
    third_ref,
    fourth_ref,
    gate_ref,
    gain_ref,
    out_ref,
    input_ref,
    gated_ref,
    *refs,
):
    weights, refs = refs[: PIECES + 1], refs[PIECES + 1 :]
    dgate_ref, dout_ref, dgain_ref = refs[:3]
    grad_ref, mixed_ref, weight_ref = refs[-3:]
    own = first_ref.shape[0]
    for at, part in enumerate((first_ref, second_ref, third_ref, fourth_ref)):
        mixed_ref[at * own : (at + 1) * own, :] = part[...]
    fill_weight(weights, weight_ref, slice(DV, 2 * DV))
    for half in range(TOTAL // SPAN):
        rows = slice(half * SPAN, (half + 1) * SPAN)
        grad_ref[rows, :] = mul(mixed_ref[rows, :], weight_ref[...])
    start = second_start(lengths_ref)
    gain = gain_ref[...]
    dgain = jnp.zeros((1, DV), F32)
    for part in range(TOTAL // PART):
        here = slice(part * PART, (part + 1) * PART)
        held = part_rows(order_ref, part)
        out = out_ref[here, :]
        gate = gate_ref[held, :]
        grad = grad_ref[held, :]
        inv = lax.rsqrt(jnp.mean(out * out, axis=1, keepdims=True) + 1e-06)
        sig = sigmoid(gate)
        swish = gate * sig
        unit = out * inv
        pulled = grad * unit
        dgate_ref[held, :] = low(pulled * gain * (sig * (1.0 + gate * (1.0 - sig))))
        dgain = dgain + jnp.sum(pulled * swish, axis=0, keepdims=True)
        inner = grad * swish * gain
        dout = inv * (inner - unit * jnp.mean(inner * unit, axis=1, keepdims=True))
        dout = jnp.where(row_limit(lengths_ref, start, part * PART, PART), dout, 0.0)
        keep_halves(dout_ref, here, halves(dout))
    dgain_ref[...] = dgain
    write_grads(refs[3:-3], [(input_ref, dgate_ref), (mixed_ref, gated_ref)])


def back_kernel(
    lengths_ref,
    order_ref,
    rates_ref,
    proj_ref,
    taps_ref,
    dout_ref,
    raw_ref,
    query_ref,
    key_ref,
    value_ref,
    state_ref,
    inverse_ref,
    reach_ref,
    fresh_ref,
    dproj_ref,
    draw_ref,
    dtaps_ref,
    drates_ref,
    dfresh_ref,
    dstate_ref,
    carry_ref,
    dq_ref,
    dk_ref,
    dv_ref,
    halo_ref,
):
    start = second_start(lengths_ref)
    rate = rates_ref[0, 0]
    bias = rates_ref[1, 0]
    masks = span_masks()
    rows, cols, same = masks
    causal = same & (rows >= cols)
    strict = same & (rows > cols)

    kept = []
    for span in range(SPANS):
        at = slice(span * SPAN, (span + 1) * SPAN)
        dout = read_halves(dout_ref, at)
        raw = raw_ref[at, :]
        beta = sigmoid(raw[:, 0:1])
        column, running, final, ratio = decay_terms(raw[:, 1:2], rate, bias, masks)
        growth = jnp.exp(running)
        tail = jnp.exp(final - running)
        key = key_ref[at, :]
        score = mul_nt(query_ref[at, :], key) * ratio
        dfresh_ref[at, :] = fine(mul_tn, halves(score), dout)
        dscore = jnp.where(causal, fine(mul_nt, dout, read_halves(fresh_ref, at)), 0.0)
        tailed = halves(tail * key.astype(F32))
        kept.append((beta, column, growth, final, tail, ratio, score, dscore, tailed))

    carry_ref[...] = jnp.zeros_like(carry_ref)
    ends = [None] * BLOCKS
    for index in reversed(range(BLOCKS)):
        at = slice(index * BLOCK, (index + 1) * BLOCK)
        low_at = index * BLOCK % SPAN
        inner = slice(low_at, low_at + BLOCK)
        beta, column, growth, final, tail, ratio, score, dscore, tailed = kept[index * BLOCK // SPAN]
        held = carry_ref[...]
        dstate = low(held)
        dstate_ref[index] = dstate
        both = mul(rows_of(tailed[0][inner], tailed[1][inner]), dstate)
        dfresh = dfresh_ref[at, :] + both[:BLOCK] + both[BLOCK:]
        dfresh_ref[at, :] = dfresh
        scale = jnp.exp(final[low_at : low_at + 1])
        if index > 0:
            read = halves(query_ref[at, :].astype(F32) * growth[inner])
            reach = read_halves(reach_ref, at)
            dout = read_halves(dout_ref, at)
            dfresh = halves(dfresh)
            gained = mul_tn(rows_of(*read, read[0]), rows_of(dout[0], dout[0], dout[1]))
            lost = mul_tn(rows_of(*reach, reach[0]), rows_of(dfresh[0], dfresh[0], dfresh[1]))
            carry_ref[...] = jnp.where(
                start == index * BLOCK, 0.0, scale * held + gained - lost
            )
        ends[index] = scale * jnp.sum(
            jnp.sum(held * state_ref[index].astype(F32), axis=0, keepdims=True), axis=1, keepdims=True
        )

    drate = jnp.zeros((1, 1), F32)
    dbias = jnp.zeros((1, 1), F32)
    steps = SPAN // BLOCK
    for span in range(SPANS):
        at = slice(span * SPAN, (span + 1) * SPAN)
        beta, column, growth, final, tail, ratio, score, dscore, tailed = kept[span]
        query = query_ref[at, :]
        key = key_ref[at, :]
        key_wide = key.astype(F32)
        dright = fine(mul_tn, read_halves(inverse_ref, at), halves(dfresh_ref[at, :]))
        dright_halves = halves(dright)
        dcouple = jnp.where(strict, -fine(mul_nt, dright_halves, read_halves(fresh_ref, at)), 0.0)
        cross = mul_nt(key, key) * ratio
        weighted = dcouple * cross
        dbeta = jnp.sum(weighted, axis=1, keepdims=True)
        ratio_grad = dscore * score + weighted * beta
        dintersect = low(dcouple * beta * ratio)
        dscored = low(dscore * ratio)
        dquery = mul(dscored, key)
        dkey = mul_tn(dscored, query) + mul(dintersect, key) + mul_tn(dintersect, key)
        pieces = [[], [], []]
        for step in range(steps):
            index = span * steps + step
            here = slice(index * BLOCK, (index + 1) * BLOCK)
            inner = slice(step * BLOCK, (step + 1) * BLOCK)
            joined = rows_of(*read_halves(dout_ref, here), *[one[inner] for one in dright_halves])
            back = mul_nt(joined, state_ref[index])
            pieces[0].append(back[:BLOCK] + back[BLOCK : 2 * BLOCK])
            pieces[1].append(back[2 * BLOCK : 3 * BLOCK] + back[3 * BLOCK :])
            back = mul_nt(rows_of(*read_halves(fresh_ref, here)), dstate_ref[index])
            pieces[2].append(back[:BLOCK] + back[BLOCK:])
        out_back, right_back, tail_back = [jnp.concatenate(piece, axis=0) for piece in pieces]
        dquery = dquery + growth * out_back
        read = jnp.sum(key_wide * right_back, axis=1, keepdims=True)
        dkey = dkey - (beta * growth) * right_back + tail * tail_back
        dbeta = (
            dbeta
            + jnp.sum(dright * value_ref[at, :].astype(F32), axis=1, keepdims=True)
            - growth * read
        )
        dgrowth = jnp.sum(query.astype(F32) * out_back, axis=1, keepdims=True) - beta * read
        dtail = tail * jnp.sum(key_wide * tail_back, axis=1, keepdims=True)
        flat = jnp.sum(
            jnp.where(rows == cols, jnp.sum(ratio_grad, axis=0, keepdims=True), 0.0),
            axis=1,
            keepdims=True,
        )
        drunning = growth * dgrowth + jnp.sum(ratio_grad, axis=1, keepdims=True) - flat - dtail
        line = jnp.sum(jnp.where(rows == cols, drunning, 0.0), axis=0, keepdims=True)
        tail_line = jnp.sum(jnp.where(rows == cols, dtail, 0.0), axis=0, keepdims=True)
        ending = jnp.concatenate(
            [jnp.broadcast_to(ends[span * steps + step], (BLOCK, 1)) for step in range(steps)],
            axis=0,
        )
        dlog = (
            jnp.sum(jnp.where(same & (rows <= cols), line, 0.0), axis=1, keepdims=True)
            + jnp.sum(jnp.where(same, tail_line, 0.0), axis=1, keepdims=True)
            + ending
        )
        raw = raw_ref[at, :]
        ddecay = -jnp.exp(rate) * dlog * sigmoid(raw[:, 1:2] + bias)
        drate = drate + jnp.sum(dlog * column, axis=0, keepdims=True)
        dbias = dbias + jnp.sum(ddecay, axis=0, keepdims=True)
        dbeta = dbeta * beta * (1.0 - beta)
        lane = lax.broadcasted_iota(jnp.int32, (SPAN, PACK), 1)
        draw = low(jnp.where(lane == 0, dbeta, jnp.where(lane == 1, ddecay, 0.0)))
        for half in range(SPAN // PART):
            held = part_rows(order_ref, span * (SPAN // PART) + half)
            draw_ref[held, :] = draw[half * PART : (half + 1) * PART]
        dq_ref[at, :] = low(dquery)
        dk_ref[at, :] = low(dkey)
        dv_ref[at, :] = low(beta * dright)
    lane = lax.broadcasted_iota(jnp.int32, (8, 128), 1)
    drates_ref[...] = jnp.where(lane == 0, drate, jnp.where(lane == 1, dbias, 0.0))

    dtaps_ref[...] = jnp.zeros_like(dtaps_ref)
    halo_ref[...] = jnp.zeros_like(halo_ref)

    def back(step, carry):
        index = BLOCKS - 1 - step
        base = pl.multiple_of(index * BLOCK, BLOCK)
        held = held_rows(order_ref, index)
        before = past_rows(order_ref, index)
        broken = (base == 0) | (base == start)
        ended = (base + BLOCK == TOTAL) | (base + BLOCK == start)
        for at in range(0, FRONT, DK):
            here = slice(at, at + DK)
            taps = taps_ref[:, here]
            halo = jnp.where(broken, 0.0, proj_ref[pl.ds(before, 8), here])
            block = proj_ref[pl.ds(held, BLOCK), here]
            joined = jnp.concatenate([halo, block], axis=0)
            shifted = [block] + [pltpu.roll(joined, offset, 0)[8:] for offset in range(1, 4)]
            conv = shifted[0] * taps[0:1]
            for offset in range(1, 4):
                conv = conv + shifted[offset] * taps[offset : offset + 1]
            sig = sigmoid(conv)
            if at >= 2 * DK:
                dact = dv_ref[pl.ds(base, BLOCK), at - 2 * DK : at - DK].astype(F32)
            else:
                act = conv * sig
                given = (dq_ref if at == 0 else dk_ref)[pl.ds(base, BLOCK), :].astype(F32)
                inv = lax.rsqrt(jnp.sum(act * act, axis=1, keepdims=True) + 1e-06)
                along = jnp.sum(act * given, axis=1, keepdims=True)
                dact = inv * (given - act * (inv * inv * along))
                if at == 0:
                    dact = dact * DK ** (-0.5)
            dconv = dact * (sig * (1.0 + conv * (1.0 - sig)))
            after = jnp.where(ended, 0.0, halo_ref[:, here])
            halo_ref[:, here] = dconv[:8]
            trailing = jnp.concatenate([dconv, after], axis=0)
            dblock = dconv * taps[0:1]
            for offset in range(1, 4):
                moved = pltpu.roll(trailing, BLOCK + 8 - offset, 0)[:BLOCK]
                dblock = dblock + moved * taps[offset : offset + 1]
            dproj_ref[pl.ds(held, BLOCK), here] = low(dblock)
            for offset in range(4):
                dtaps_ref[offset : offset + 1, here] += jnp.sum(
                    dconv * shifted[offset], axis=0, keepdims=True
                )
        return carry

    lax.fori_loop(0, BLOCKS, back, 0)


def entry_kernel(
    query_ref,
    key_ref,
    value_ref,
    beta_ref,
    decay_ref,
    norm_ref,
    ffn_ref,
    query_conv_ref,
    key_conv_ref,
    value_conv_ref,
    gain_ref,
    out_ref,
    small_ref,
):
    rows = query_ref.shape[0]
    wide = query_ref.shape[1]
    out_ref[:rows, :wide] = query_ref[...]
    out_ref[:rows, wide : 2 * wide] = key_ref[...]
    out_ref[:rows, 2 * wide :] = value_ref[...]
    small_ref[...] = jnp.zeros_like(small_ref)
    for at, line in enumerate((beta_ref, decay_ref, norm_ref, ffn_ref)):
        small_ref[at : at + 1, :] = line[...].astype(F32)
    taps = query_conv_ref.shape[0]
    cols = 0
    for conv in (query_conv_ref, key_conv_ref, value_conv_ref):
        small_ref[4 : 4 + taps, cols : cols + conv.shape[1]] = conv[...].astype(F32)
        cols += conv.shape[1]
    small_ref[8:9, : gain_ref.shape[1]] = gain_ref[...].astype(F32)
    out_ref[rows:, :] = jnp.zeros((PACK, out_ref.shape[1]), BF16)
    out_ref[rows:, :rows] = low(small_ref[...])


def pack_kernel(behind_ref, *refs):
    packs = refs[:PIECES]
    norm_ref, ffn_ref, small_ref, taps_ref, gain_ref, all_ref = refs[PIECES:]
    share = packs[0].shape[1]
    for d, pack in enumerate(packs):
        here = slice(d * share, (d + 1) * share)
        small_ref[:, here] = pack[...]
        wide = pack[...].astype(F32)
        all_ref[d] = wide
        norm_ref[:, here] = wide[2:3]
        ffn_ref[:, here] = wide[3:4]
    narrow = DK // PIECES
    for n in range(PIECES):
        wide = all_ref[behind_ref[n]]
        taps_ref[:, n * narrow : (n + 1) * narrow] = wide[4:8, :narrow]
        taps_ref[:, DK + n * narrow : DK + (n + 1) * narrow] = wide[4:8, narrow : 2 * narrow]
        at = 2 * DK + n * 2 * narrow
        taps_ref[:, at : at + 2 * narrow] = wide[4:8, 2 * narrow :]
        gain_ref[:, n * 2 * narrow : (n + 1) * 2 * narrow] = wide[8:9, : 2 * narrow]


def pack_call(behind, pieces, share, width):
    rows = [share // PACK] * (PIECES + 1)
    rows[MIDDLE + 1] = share // 2 // PACK
    picked = [d for d in range(PIECES + 1) if d != MIDDLE]

    def block(at):
        return pl.BlockSpec((PACK, share), lambda i: (at, 0))

    line = jax.ShapeDtypeStruct((1, width), F32)
    whole = lambda shape: pl.BlockSpec(shape, lambda i: (0, 0))
    shapes = (
        line,
        line,
        jax.ShapeDtypeStruct((PACK, width), BF16),
        jax.ShapeDtypeStruct((4, FRONT), F32),
        jax.ShapeDtypeStruct((1, DV), F32),
    )
    return pl.pallas_call(
        pack_kernel,
        grid=(1,),
        out_shape=shapes,
        in_specs=[pl.BlockSpec(memory_space=SMEM)] + [block(rows[d]) for d in picked],
        out_specs=tuple(whole(one.shape) for one in shapes),
        scratch_shapes=[pltpu.VMEM((PIECES, PACK, share), F32)],
        name="pack",
    )(behind, *[pieces[d] for d in picked])


def run_kernel(kernel, name, scalars, arrays, results, scratch, cost):
    return pl.pallas_call(
        kernel,
        out_shape=tuple(jax.ShapeDtypeStruct(shape, kind) for shape, kind in results),
        in_specs=[pl.BlockSpec(memory_space=SMEM)] * len(scalars)
        + [pl.BlockSpec(memory_space=VMEM)] * len(arrays),
        out_specs=tuple([pl.BlockSpec(memory_space=VMEM)] * len(results)),
        scratch_shapes=[pltpu.VMEM(shape, kind) for shape, kind in scratch],
        compiler_params=pltpu.CompilerParams(vmem_limit_bytes=LIMIT),
        cost_estimate=pl.CostEstimate(
            flops=cost * 1_000_000_000, bytes_accessed=8_000_000, transcendentals=1_000_000
        ),
        name=name,
    )(*scalars, *arrays)


def front_call(lengths, order, rates, taps, rows, small, pieces):
    results = (
        ((TOTAL, FRONT), F32),
        ((TOTAL, DK), BF16),
        ((TOTAL, DK), BF16),
        ((TOTAL, DV), BF16),
        ((TOTAL, PACK), F32),
        ((TOTAL, 2 * SPAN), BF16),
        ((TOTAL, 2 * DK), BF16),
        ((TOTAL, DV), F32),
        ((TOTAL, 2 * DK), BF16),
        ((TOTAL, 2 * SPAN), BF16),
        ((TOTAL, 128), F32),
    )
    return run_kernel(
        front_kernel,
        "mixer_front",
        (lengths, order, rates),
        (taps, rows, small, *pieces),
        results,
        (((rows.shape[1], FRONT), BF16),),
        15,
    )


def chain_call(lengths, arrays):
    results = (((BLOCKS, DK, DV), BF16), ((TOTAL, 2 * DV), BF16), ((TOTAL, DV), F32))
    return run_kernel(
        chain_kernel, "mixer_chain", (lengths,), arrays, results, (((DK, DV), F32),), 7
    )


def gate_call(order, arrays, width):
    half = ((SPAN, width), BF16)
    results = (((TOTAL, DV), F32), ((TOTAL, DV), BF16), half, half)
    return run_kernel(
        gate_kernel, "mixer_gate", (order,), arrays, results, (((width, 2 * DV), BF16),), 6
    )


def gate_back_call(lengths, order, arrays, shapes, width):
    scratch = (((TOTAL, DV), F32), ((TOTAL, width), BF16), ((width, DV), BF16))
    results = (((TOTAL, DV), BF16), ((TOTAL, 2 * DV), BF16), ((1, DV), F32), *shapes)
    return run_kernel(
        gate_back_kernel, "gate_back", (lengths, order), arrays, results, scratch, 7
    )


def back_call(lengths, order, rates, arrays):
    results = (
        ((TOTAL, FRONT), BF16),
        ((TOTAL, PACK), BF16),
        ((4, FRONT), F32),
        ((8, 128), F32),
    )
    scratch = (
        ((TOTAL, DV), F32),
        ((BLOCKS, DK, DV), BF16),
        ((DK, DV), F32),
        ((TOTAL, DK), BF16),
        ((TOTAL, DK), BF16),
        ((TOTAL, DV), BF16),
        ((8, FRONT), F32),
    )
    return run_kernel(
        back_kernel, "mixer_back", (lengths, order, rates), arrays, results, scratch, 17
    )


def plain_product(left, right):
    return jnp.dot(left, right, preferred_element_type=F32)


def transposed_product(left, right):
    return lax.dot_general(left, right, (((0,), (0,)), ((), ())), preferred_element_type=F32)


def product_back(grad, weight):
    return lax.dot_general(grad, weight, (((1,), (1,)), ((), ())), preferred_element_type=F32)


def piece_shapes(width, share):
    full = ((share, width), BF16)
    half = ((share // 2, width), BF16)
    return [half if d in (MIDDLE, MIDDLE + 1) else full for d in range(PIECES + 1)]


def cut_rows(whole):
    share = whole.shape[0] // PIECES
    middle = MIDDLE * share
    cuts = [d * share for d in range(MIDDLE + 1)] + [middle + share // 2]
    cuts += [d * share for d in range(MIDDLE + 1, PIECES + 1)]
    return [whole[a:b] for a, b in zip(cuts[:-1], cuts[1:])]


class Ring:
    def __init__(self, count):
        self.count = count
        self.circle = count == PIECES
        if self.circle:
            self.order = list(range(0, count, 2)) + list(range(count - 1, 0, -2))
            place = [self.order.index(i) for i in range(count)]
            ahead = [[self.order[(place[i] + d) % count] for d in range(count)] for i in range(count)]
            behind = [[(place[j] - place[i]) % count for j in range(count)] for i in range(count)]
            here = lax.axis_index("dp")
            self.ahead = jnp.array(ahead, jnp.int32)[here]
            self.behind = jnp.array(behind, jnp.int32)[here]
        else:
            self.ahead = jnp.arange(PIECES, dtype=jnp.int32)

    def step(self, value, places):
        pairs = [
            (self.order[i], self.order[(i + places) % self.count]) for i in range(self.count)
        ]
        return lax.ppermute(value, "dp", pairs)


class Gather:
    def __init__(self, ring, part, share):
        self.ring, self.part, self.share = ring, part, share
        self.flight = (part, part)
        self.steps = []
        if not ring.circle:
            self.whole = lax.all_gather(part, "dp", axis=0)

    def hop(self):
        if not self.ring.circle:
            return
        up, down = self.flight
        if len(self.steps) == MIDDLE - 1:
            up, down = up[: self.share // 2], down[self.share // 2 :]
        self.flight = (self.ring.step(up, 1), self.ring.step(down, -1))
        self.steps.append(self.flight)

    def held(self):
        return self.flight if self.ring.circle else ()

    def take(self, flight):
        if self.ring.circle:
            self.flight = flight
            self.steps[-1] = flight

    def pieces(self):
        if not self.ring.circle:
            return cut_rows(self.whole[:, : self.share].reshape(-1, self.whole.shape[2]))
        *full, last = self.steps
        return [self.part, *[down for _, down in full], *last, *[up for up, _ in reversed(full)]]

    def packs(self):
        if not self.ring.circle:
            return self.whole[:, self.share :, : self.share]
        rows = self.pieces()
        half = self.share // 2
        packs = [piece[self.share :, : self.share] for piece in rows]
        packs[MIDDLE + 1] = rows[MIDDLE + 1][half:, : self.share]
        return jnp.stack(packs[:MIDDLE] + packs[MIDDLE + 1 :])


class Scatter:
    def __init__(self, ring, up, down):
        self.ring, self.first = ring, (up, down)
        self.flight = ()
        self.left = MIDDLE

    def rest(self, pieces):
        self.pieces = [*pieces[:MIDDLE], *self.first, *pieces[MIDDLE:]]
        if not self.ring.circle:
            whole = jnp.concatenate(self.pieces, axis=0)
            self.whole = lax.psum_scatter(whole, "dp", scatter_dimension=0, tiled=True)

    def hop(self):
        if not self.ring.circle:
            return
        if self.left == MIDDLE:
            up, down = self.first
        else:
            pieces = self.pieces
            ahead = pieces[self.left].astype(F32)
            back = pieces[len(pieces) - self.left].astype(F32)
            up, down = [one.astype(F32) for one in self.flight]
            cut = up.shape[0]
            if self.left == MIDDLE - 1:
                up = jnp.concatenate([ahead[:cut] + up, ahead[cut:]], axis=0)
                down = jnp.concatenate([back[:cut], back[cut:] + down], axis=0)
            else:
                up = ahead + up
                down = back + down
            up, down = low(up), low(down)
        self.flight = (self.ring.step(up, 1), self.ring.step(down, -1))
        self.left -= 1

    def held(self):
        return self.flight

    def take(self, flight):
        self.flight = flight


def finish_kernel(first_ref, up_ref, down_ref, *outs):
    total = first_ref[...].astype(F32) + up_ref[...].astype(F32) + down_ref[...].astype(F32)
    rows = first_ref.shape[0]
    at = 0
    for out in outs:
        turned = out.shape[0] != rows
        width = out.shape[0] if turned else out.shape[1]
        piece = total[:, at : at + width]
        out[...] = piece.T if turned else piece
        at += width


def finish(sums, shapes):
    if not sums.ring.circle:
        total = sums.whole.astype(F32)
        outs, at = [], 0
        for shape in shapes:
            turned = shape[0] != total.shape[0]
            width = shape[0] if turned else shape[1]
            piece = total[:, at : at + width]
            outs.append(piece.T if turned else piece)
            at += width
        return outs
    return run_kernel(
        finish_kernel,
        "finish",
        (),
        (sums.pieces[0], *sums.flight),
        [(shape, F32) for shape in shapes],
        (),
        2,
    )


def sync(moving, *values):
    flights, values = lax.optimization_barrier(([one.held() for one in moving], values))
    for one, flight in zip(moving, flights):
        one.take(flight)
    return values


def swap(value, distance):
    count = lax.axis_size("tensor")
    return lax.ppermute(value, "tensor", [(i, i ^ distance) for i in range(count)])


def folded(keep, near):
    own = keep.shape[0] // 2
    return low(keep[own:].astype(F32) + near[own:].astype(F32))


def local(
    tokens,
    lengths,
    cotangent,
    norm_gain,
    query_weight,
    key_weight,
    value_weight,
    gate_weight,
    beta_weight,
    decay_weight,
    query_conv,
    key_conv,
    value_conv,
    decay_params,
    head_gain,
    out_weight,
    ffn_gain,
    ffn_gate,
    ffn_up,
    ffn_down,
):
    count = lax.axis_size("dp")
    team = lax.axis_size("tensor")
    ring = Ring(count)
    ahead = ring.ahead
    place = lax.axis_index("tensor")
    swapped = [[[0, 2, 1, 3][i ^ t] for i in range(team)] for t in range(team)]
    order = jnp.array(swapped, jnp.int32)[place]
    share = norm_gain.shape[0]
    narrow = head_gain.shape[0]
    narrow_q = query_conv.shape[1]
    cuts = (0, narrow_q, 2 * narrow_q, share)
    width = tokens.shape[1]
    hidden = ffn_gate.shape[1]
    own = tokens.shape[0]
    low_rows = ((own, width), BF16)
    wide_rows = ((own, width), F32)
    wide_line = ((1, width), F32)

    padded = -(-3 * hidden // 128) * 128
    half_rows = ((SPAN, width), BF16)
    entry = pl.pallas_call(
        entry_kernel,
        out_shape=jax.ShapeDtypeStruct((share + PACK, FRONT), BF16),
        scratch_shapes=[pltpu.VMEM((PACK, share), F32)],
        name="entry",
    )(
        query_weight,
        key_weight,
        value_weight,
        beta_weight.reshape(1, share),
        decay_weight.reshape(1, share),
        norm_gain.reshape(1, share),
        ffn_gain.reshape(1, share),
        query_conv,
        key_conv,
        value_conv,
        head_gain.reshape(1, narrow),
    )
    entries = Gather(ring, entry, share)
    entries.hop()
    tokens_2, tokens_1, cotangent, out_weight, gate_weight, ffn_gate, ffn_up, ffn_down = sync(
        [entries],
        swap(tokens, 2),
        swap(tokens, 1),
        cotangent,
        out_weight,
        gate_weight,
        ffn_gate,
        ffn_up,
        ffn_down,
    )
    entries.hop()
    tokens_3, grads_2, grads_1, side, ffn_gate, ffn_up, ffn_down = sync(
        [entries],
        swap(tokens_2, 1),
        swap(cotangent, 2),
        swap(cotangent, 1),
        jnp.concatenate([gate_weight, out_weight.T], axis=1),
        ffn_gate,
        ffn_up,
        ffn_down,
    )
    entries.hop()
    blank = jnp.zeros((share, padded - 3 * hidden), BF16)
    grads_3, side, wide = sync(
        [entries],
        swap(grads_2, 1),
        side,
        jnp.concatenate([ffn_gate, ffn_up, ffn_down.T, blank], axis=1),
    )
    sides = Gather(ring, side, share)
    entries.hop()
    sides.hop()
    (wide,) = sync([entries, sides], wide)

    sides.hop()
    entry_pieces = entries.pieces()
    if ring.circle:
        norm_whole, ffn_gain_whole, small, taps, gains = pack_call(
            ring.behind, entry_pieces, share, width
        )
    else:
        packs = jnp.swapaxes(entries.packs(), 0, 1)
        norm_whole = packs[2].reshape(1, width).astype(F32)
        ffn_gain_whole = packs[3].reshape(1, width).astype(F32)
        small = packs.reshape(PACK, width)
        packs = packs[4:9].astype(F32)
        taps = jnp.concatenate(
            [packs[:4, :, a:b].reshape(4, -1) for a, b in zip(cuts[:-1], cuts[1:])], axis=1
        )
        gains = packs[4, :, :narrow].reshape(1, DV)
    mixer_input, down_grad = run_kernel(
        gather_kernel,
        "gather",
        (ahead,),
        (norm_whole, tokens, tokens_2, tokens_1, tokens_3, cotangent, grads_2, grads_1, grads_3),
        (((TOTAL, width), BF16), ((TOTAL, width), BF16)),
        (low_rows,),
        4,
    )
    mixer_input, down_grad, taps, gains, small, ffn_gain_whole, norm_whole, wide = sync(
        [sides], mixer_input, down_grad, taps, gains, small, ffn_gain_whole, norm_whole, wide
    )

    wides = Gather(ring, wide, share)
    sides.hop()
    wides.hop()
    front = front_call(lengths, order, decay_params, taps, mixer_input, small, entry_pieces)
    proj, query, key, value, raw, inverse, reach, base, tail, score, growth = sync(
        [sides, wides], *front
    )

    sides.hop()
    wides.hop()
    state, fresh, out = sync(
        [sides], *chain_call(lengths, (query, reach, base, tail, score, growth))
    )
    side_pieces = sides.pieces()
    gate, gated, keep, send = sync(
        [wides], *gate_call(order, (out, gains, mixer_input, *side_pieces), width)
    )
    wides.hop()
    near, keep = sync([], swap(send, 1), keep)
    far, keep, near = sync([wides], swap(folded(keep, near), 2), keep, near)

    wides.hop()
    middle, second = run_kernel(
        middle_kernel,
        "middle",
        (ahead,),
        (tokens, keep, near, far, ffn_gain_whole),
        (wide_rows, low_rows),
        (low_rows,),
        2,
    )
    middle, second, second_2, second_1 = sync(
        [], middle, second, swap(second, 2), swap(second, 1)
    )
    (second_3,) = sync([wides], swap(second_2, 1))

    ffn_pieces = wides.pieces()
    ffn_input, out_keep, out_send, keep, send, product, grad_acts, grads_up, grads_down = sync(
        [],
        *run_kernel(
            ffn_kernel,
            "ffn",
            (),
            (down_grad, second, second_2, second_1, second_3, *ffn_pieces),
            (
                ((TOTAL, width), BF16),
                half_rows,
                half_rows,
                half_rows,
                half_rows,
                ((TOTAL, hidden), BF16),
                ((TOTAL, 2 * hidden), BF16),
                *piece_shapes(padded, width // PIECES)[MIDDLE : MIDDLE + 2],
            ),
            (((width, 3 * hidden), BF16),),
            13,
        ),
    )

    ffn_sums = Scatter(ring, grads_up, grads_down)
    ffn_sums.hop()
    shapes = piece_shapes(padded, width // PIECES)
    near, keep, out_keep, out_send, *ffn_grads = sync(
        [ffn_sums],
        swap(send, 1),
        keep,
        out_keep,
        out_send,
        *run_kernel(
            ffn_grads_kernel,
            "ffn_grads",
            (),
            (ffn_input, grad_acts, down_grad, product),
            shapes[:MIDDLE] + shapes[MIDDLE + 2 :],
            (),
            7,
        ),
    )
    ffn_sums.rest(ffn_grads)
    ffn_sums.hop()
    far, keep, near, out_keep, out_near = sync(
        [], swap(folded(keep, near), 2), keep, near, out_keep, swap(out_send, 1)
    )

    grad_middle, grad_mixed, dffn_gain = run_kernel(
        middle_back_kernel,
        "middle_back",
        (ahead,),
        (cotangent, middle, keep, near, far, ffn_gain_whole),
        (wide_rows, low_rows, wide_line),
        (low_rows,),
        3,
    )
    grad_middle, grad_mixed, dffn_gain, mixed_2, mixed_1, out_keep, out_near = sync(
        [ffn_sums],
        grad_middle,
        grad_mixed,
        dffn_gain,
        swap(grad_mixed, 2),
        swap(grad_mixed, 1),
        out_keep,
        out_near,
    )

    ffn_sums.hop()
    dgate, dout, dgain, *side_grads = gate_back_call(
        lengths,
        order,
        (
            grad_mixed,
            mixed_2,
            mixed_1,
            swap(mixed_2, 1),
            gate,
            gains,
            out,
            mixer_input,
            gated,
            *side_pieces,
        ),
        piece_shapes(2 * DV, width // PIECES),
        width,
    )
    dgate, dout, dgain, out_keep, out_near, *side_grads = sync(
        [ffn_sums], dgate, dout, dgain, out_keep, out_near, *side_grads
    )

    ffn_sums.hop()
    side_sums = Scatter(ring, *side_grads[MIDDLE : MIDDLE + 2])
    side_sums.rest(side_grads[:MIDDLE] + side_grads[MIDDLE + 2 :])
    side_sums.hop()
    out_far = swap(folded(out_keep, out_near), 2)
    dproj, draw, dtaps, drates, out_far, out_keep, out_near = sync(
        [ffn_sums, side_sums],
        *back_call(
            lengths,
            order,
            decay_params,
            (proj, taps, dout, raw, query, key, value, state, inverse, reach, fresh),
        ),
        out_far,
        out_keep,
        out_near,
    )

    side_sums.hop()
    keep, send, dnorm, dtaps, dgain, drates, dffn_gain, out_far, *entry_grads = sync(
        [side_sums, ffn_sums],
        *run_kernel(
            input_back_kernel,
            "input_back",
            (ahead,),
            (
                dproj,
                dgate,
                draw,
                small,
                tokens,
                tokens_2,
                tokens_1,
                tokens_3,
                *entry_pieces,
                *side_pieces,
            ),
            (half_rows, half_rows, wide_line),
            (low_rows, ((width, FRONT), BF16), ((width, DV), BF16)),
            6,
        ),
        dtaps,
        dgain,
        drates,
        dffn_gain,
        out_far,
        *run_kernel(
            entry_grads_kernel,
            "entry_grads",
            (),
            (mixer_input, dproj),
            piece_shapes(FRONT, width // PIECES),
            (),
            5,
        ),
    )

    side_sums.hop()
    entry_sums = Scatter(ring, *entry_grads[MIDDLE : MIDDLE + 2])
    entry_sums.rest(entry_grads[:MIDDLE] + entry_grads[MIDDLE + 2 :])
    entry_sums.hop()
    lines = jnp.concatenate([dnorm, dffn_gain], axis=0)
    near, keep, lines, dtaps, dgain, drates, out_far = sync(
        [side_sums, entry_sums, ffn_sums],
        swap(send, 1),
        keep,
        lines + swap(lines, 1),
        dtaps,
        dgain,
        drates,
        out_far,
    )

    side_sums.hop()
    entry_sums.hop()
    channel_grads = jnp.concatenate(
        [
            dtaps[:, a * count : b * count].reshape(4, count, b - a)
            for a, b in zip(cuts[:-1], cuts[1:])
        ],
        axis=2,
    )
    gain_grads = jnp.pad(dgain.reshape(1, count, narrow), ((0, 0), (0, 0), (0, share - narrow)))
    channel_grads = jnp.concatenate([channel_grads, gain_grads], axis=0)
    if ring.circle:
        channel_grads = channel_grads[:, ahead]
    pack_grad = jnp.concatenate(
        [
            transposed_product(draw, mixer_input)[:2],
            lines + swap(lines, 2),
            channel_grads.reshape(5, width),
            jnp.broadcast_to(drates[0:1, 0:1], (1, width)),
            jnp.broadcast_to(drates[0:1, 1:2], (1, width)),
            jnp.zeros((PACK - 11, width), F32),
        ],
        axis=0,
    )
    far, keep, near, pack_grad, out_far = sync(
        [side_sums, entry_sums, ffn_sums],
        swap(folded(keep, near), 2),
        keep,
        near,
        pack_grad,
        out_far,
    )

    def pack_steps(places):
        if not ring.circle:
            return []
        return [ring.step(pack_grad[:, d * share : (d + 1) * share], d) for d in places]

    entry_sums.hop()
    ffn_outs = finish(ffn_sums, ((share, hidden), (share, hidden), (hidden, share)))
    tokens_grad, dgate_weight, dup_weight, ddown_weight, out_far, pack_grad, *packs_1 = sync(
        [side_sums, entry_sums],
        run_kernel(
            tokens_back_kernel,
            "tokens_back",
            (ahead,),
            (tokens, grad_middle, keep, near, far, norm_whole),
            (wide_rows,),
            (low_rows,),
            3,
        )[0],
        *ffn_outs,
        out_far,
        pack_grad,
        *pack_steps((1, 2, 3)),
    )

    entry_sums.hop()
    side_outs = finish(side_sums, ((share, DV), (DV, share)))
    block_out, dside_weight, dout_weight, pack_grad, *packs_2 = sync(
        [entry_sums],
        run_kernel(
            block_out_kernel,
            "block_out",
            (ahead,),
            (middle, out_keep, out_near, out_far),
            (low_rows,),
            (),
            3,
        )[0],
        *side_outs,
        pack_grad,
        *pack_steps((4, 5, 6, 7)),
    )

    if ring.circle:
        pack_sum = pack_grad[:, :share]
        for one in (*packs_1, *packs_2):
            pack_sum = pack_sum + one
    else:
        pack_sum = lax.psum_scatter(pack_grad, "dp", scatter_dimension=1, tiled=True)
    query_out, key_out, value_out = finish(entry_sums, ((share, DK), (share, DK), (share, DV)))
    return (
        block_out,
        tokens_grad,
        pack_sum[2],
        query_out,
        key_out,
        value_out,
        dside_weight,
        pack_sum[0][:, None],
        pack_sum[1][:, None],
        pack_sum[4:8, cuts[0] : cuts[1]],
        pack_sum[4:8, cuts[1] : cuts[2]],
        pack_sum[4:8, cuts[2] : cuts[3]],
        pack_sum[9:11, 0:1],
        pack_sum[8, :narrow],
        dout_weight,
        pack_sum[3],
        dgate_weight,
        dup_weight,
        ddown_weight,
    )


def solution(mesh):
    rows = P(("dp", "tensor"), None)
    weight = P("dp", "tensor")
    channel = P(None, ("tensor", "dp"))
    down = P("tensor", "dp")
    return jax.shard_map(
        local,
        mesh=mesh,
        in_specs=(
            rows,
            P("dp", None),
            rows,
            P("dp"),
            weight,
            weight,
            weight,
            weight,
            weight,
            weight,
            channel,
            channel,
            channel,
            P(None, "tensor"),
            P(("tensor", "dp")),
            down,
            P("dp"),
            weight,
            weight,
            down,
        ),
        out_specs=(
            rows,
            rows,
            P("dp"),
            weight,
            weight,
            weight,
            weight,
            weight,
            weight,
            channel,
            channel,
            channel,
            P(None, "tensor"),
            P(("tensor", "dp")),
            down,
            P("dp"),
            weight,
            weight,
            down,
        ),
        check_vma=False,
    )
```

```python
import jax
import jax.numpy as jnp
from jax import lax
from jax.experimental import pallas as pl
from jax.experimental.pallas import tpu as pltpu
from jax.sharding import PartitionSpec as P

DK = 256
DV = 512
BLOCK = 64
SPAN = 256
PART = 128
TOTAL = 512
FRONT = 2 * DK + DV
PACK = 16
PIECES = 8
MIDDLE = PIECES // 2
BLOCKS = TOTAL // BLOCK
SPANS = TOTAL // SPAN
F32 = jnp.float32
BF16 = jnp.bfloat16
SMEM = pltpu.SMEM
VMEM = pltpu.VMEM
LIMIT = 56 * 1024 * 1024


def mul(left, right):
    return lax.dot_general(left, right, (((1,), (0,)), ((), ())), preferred_element_type=F32)


def mul_nt(left, right):
    return lax.dot_general(left, right, (((1,), (1,)), ((), ())), preferred_element_type=F32)


def mul_tn(left, right):
    return lax.dot_general(left, right, (((0,), (0,)), ((), ())), preferred_element_type=F32)


def low(value):
    return value.astype(BF16)


def halves(value):
    high = low(value)
    return high, low(value - high.astype(F32))


def fine(product, left, right):
    return product(left[0], right[0]) + (product(left[0], right[1]) + product(left[1], right[0]))


def mul_fine(left, right):
    return fine(mul, halves(left), halves(right))


def keep_halves(ref, at, pair):
    width = pair[0].shape[1]
    ref[at, :width] = pair[0]
    ref[at, width:] = pair[1]


def read_halves(ref, at):
    width = ref.shape[1] // 2
    return ref[at, :width], ref[at, width:]


def rows_of(*values):
    return jnp.concatenate(values, axis=0)


def sigmoid(value):
    return 1.0 / (1.0 + jnp.exp(-value))


def softplus(value):
    return jnp.maximum(value, 0.0) + jnp.log1p(jnp.exp(-jnp.abs(value)))


def span_masks():
    rows = lax.broadcasted_iota(jnp.int32, (SPAN, SPAN), 0)
    cols = lax.broadcasted_iota(jnp.int32, (SPAN, SPAN), 1)
    same = (rows // BLOCK) == (cols // BLOCK)
    return rows, cols, same


def decay_terms(raw, rate, bias, masks):
    rows, cols, same = masks
    causal = same & (rows >= cols)
    column = -jnp.exp(rate) * softplus(raw + bias)
    line = jnp.sum(jnp.where(rows == cols, column, 0.0), axis=0, keepdims=True)
    running = jnp.sum(jnp.where(causal, line, 0.0), axis=1, keepdims=True)
    running_line = jnp.sum(jnp.where(same & (rows <= cols), column, 0.0), axis=0, keepdims=True)
    final = jnp.sum(jnp.where(same, line, 0.0), axis=1, keepdims=True)
    ratio = jnp.where(causal, jnp.exp(jnp.where(causal, running - running_line, 0.0)), 0.0)
    return column, running, final, ratio


def unit_inverse(coupling, masks):
    rows, cols, same = masks
    inverse = jnp.where(rows == cols, 1.0, 0.0) - jnp.where(
        (rows // 2 == cols // 2), coupling, 0.0
    )
    width = 2
    while width < BLOCK:
        inner = (rows // (2 * width) == cols // (2 * width)) & (rows // width != cols // width)
        part = jnp.where(inner, coupling, 0.0)
        inverse = inverse - mul_fine(mul_fine(inverse, part), inverse)
        width = width * 2
    return inverse


def second_start(lengths_ref):
    return (lengths_ref[0, 0] + BLOCK - 1) // BLOCK * BLOCK


def held_rows(order_ref, index):
    half = index % 2
    return pl.multiple_of(order_ref[index // 2] * PART + half * BLOCK, BLOCK)


def part_rows(order_ref, index):
    return pl.ds(pl.multiple_of(order_ref[index] * PART, PART), PART)


def past_rows(order_ref, index):
    return pl.multiple_of(held_rows(order_ref, jnp.maximum(index - 1, 0)) + BLOCK - 8, 8)


def row_limit(lengths_ref, start, base, count):
    place = lax.broadcasted_iota(jnp.int32, (count, 1), 0) + base
    limit = jnp.where(place >= start, start + lengths_ref[0, 1], lengths_ref[0, 0])
    return place < limit


def fill_weight(pieces, weight_ref, cols):
    at = 0
    total = weight_ref.shape[0]
    middle = (len(pieces) - 1) // 2
    share = total // (len(pieces) - 1)
    for index, piece in enumerate(pieces):
        count = share // 2 if index in (middle, middle + 1) else share
        weight_ref[at : at + count, :] = piece[:count, cols]
        at += count


def norm_of(rows, gain):
    return low(rows * lax.rsqrt(jnp.mean(rows * rows, axis=1, keepdims=True) + 1e-06) * gain)


def ahead_copy(ahead_ref, source_ref, target_ref, rows):
    count = ahead_ref.shape[0]
    share = target_ref.shape[1] // count
    for d in range(count):
        cols = pl.ds(pl.multiple_of(ahead_ref[d] * share, share), share)
        target_ref[rows, d * share : (d + 1) * share] = source_ref[:, cols]


def gather_kernel(ahead_ref, norm_ref, *refs):
    input_ref, grad_ref, wide_ref = refs[-3:]
    size = wide_ref.shape[0]
    for at in range(4):
        rows = slice(at * size, (at + 1) * size)
        ahead_copy(ahead_ref, refs[at], wide_ref, slice(None))
        ahead_copy(ahead_ref, refs[4 + at], grad_ref, rows)
        input_ref[rows, :] = norm_of(wide_ref[...].astype(F32), norm_ref[...])


def front_kernel(
    lengths_ref,
    order_ref,
    rates_ref,
    taps_ref,
    input_ref,
    small_ref,
    *refs,
):
    pieces = refs[:-12]
    (
        proj_ref,
        query_ref,
        key_ref,
        value_ref,
        raw_ref,
        inverse_ref,
        reach_ref,
        base_ref,
        tail_ref,
        score_ref,
        growth_ref,
        weight_ref,
    ) = refs[-12:]
    fill_weight(pieces, weight_ref, slice(0, FRONT))
    for half in range(TOTAL // SPAN):
        rows = slice(half * SPAN, (half + 1) * SPAN)
        proj_ref[rows, :] = mul(input_ref[rows, :], weight_ref[...])
    start = second_start(lengths_ref)
    rate = rates_ref[0, 0]
    bias = rates_ref[1, 0]

    def front(index, carry):
        base = pl.multiple_of(index * BLOCK, BLOCK)
        held = held_rows(order_ref, index)
        before = past_rows(order_ref, index)
        broken = (base == 0) | (base == start)
        for at in range(0, FRONT, DK):
            here = slice(at, at + DK)
            taps = taps_ref[:, here]
            halo = jnp.where(broken, 0.0, proj_ref[pl.ds(before, 8), here])
            block = proj_ref[pl.ds(held, BLOCK), here]
            joined = jnp.concatenate([halo, block], axis=0)
            conv = block * taps[0:1]
            for offset in range(1, 4):
                conv = conv + pltpu.roll(joined, offset, 0)[8:] * taps[offset : offset + 1]
            act = conv * sigmoid(conv)
            if at >= 2 * DK:
                value_ref[pl.ds(base, BLOCK), at - 2 * DK : at - DK] = low(act)
            else:
                inv = lax.rsqrt(jnp.sum(act * act, axis=1, keepdims=True) + 1e-06)
                if at == 0:
                    query_ref[pl.ds(base, BLOCK), :] = low(act * inv * DK ** (-0.5))
                else:
                    key_ref[pl.ds(base, BLOCK), :] = low(act * inv)
        return carry

    lax.fori_loop(0, BLOCKS, front, 0)
    for part in range(TOTAL // PART):
        raw_ref[part * PART : (part + 1) * PART, :] = mul_nt(
            input_ref[part_rows(order_ref, part), :], small_ref[...]
        )

    masks = span_masks()
    rows, cols, same = masks
    strict = same & (rows > cols)
    lane = lax.broadcasted_iota(jnp.int32, (SPAN, 128), 1)
    for span in range(SPANS):
        at = slice(span * SPAN, (span + 1) * SPAN)
        raw = raw_ref[at, :]
        beta = sigmoid(raw[:, 0:1])
        _, running, final, ratio = decay_terms(raw[:, 1:2], rate, bias, masks)
        growth = jnp.exp(running)
        key = key_ref[at, :]
        coupling = jnp.where(strict, beta * mul_nt(key, key) * ratio, 0.0)
        inverse = halves(unit_inverse(coupling, masks))
        keep_halves(inverse_ref, at, inverse)
        key_wide = key.astype(F32)
        base_ref[at, :] = fine(mul, inverse, halves(beta * value_ref[at, :].astype(F32)))
        reach = fine(mul, inverse, halves(beta * growth * key_wide))
        keep_halves(reach_ref, at, halves(reach))
        keep_halves(tail_ref, at, halves(jnp.exp(final - running) * key_wide))
        keep_halves(score_ref, at, halves(mul_nt(query_ref[at, :], key) * ratio))
        growth_ref[at, :] = jnp.where(lane == 0, growth, jnp.exp(final))


def chain_kernel(
    lengths_ref,
    query_ref,
    reach_ref,
    base_ref,
    tail_ref,
    score_ref,
    growth_ref,
    state_ref,
    fresh_ref,
    out_ref,
    carry_ref,
):
    start = second_start(lengths_ref)
    carry_ref[...] = jnp.zeros_like(carry_ref)
    for index in range(BLOCKS):
        at = slice(index * BLOCK, (index + 1) * BLOCK)
        held = jnp.where(start == index * BLOCK, 0.0, carry_ref[...])
        state = low(held)
        state_ref[index] = state
        both = mul(rows_of(*read_halves(reach_ref, at), query_ref[at, :]), state)
        fresh = halves(base_ref[at, :] - both[:BLOCK] - both[BLOCK : 2 * BLOCK])
        keep_halves(fresh_ref, at, fresh)
        out_ref[at, :] = growth_ref[at, 0:1] * both[2 * BLOCK :]
        if index + 1 < BLOCKS:
            final = growth_ref[index * BLOCK : index * BLOCK + 1, 1:2]
            tail = read_halves(tail_ref, at)
            carry_ref[...] = final * held + mul_tn(
                rows_of(*tail, tail[0]), rows_of(fresh[0], fresh[0], fresh[1])
            )

    for part in range(TOTAL // PART):
        span = part * PART // SPAN
        here = slice(part * PART, (part + 1) * PART)
        fresh = read_halves(fresh_ref, slice(span * SPAN, (span + 1) * SPAN))
        out = out_ref[here, :] + fine(mul, read_halves(score_ref, here), fresh)
        out_ref[here, :] = jnp.where(row_limit(lengths_ref, start, part * PART, PART), out, 0.0)


def gate_kernel(order_ref, out_ref, gain_ref, input_ref, *refs):
    pieces = refs[:-5]
    gate_ref, gated_ref, keep_ref, send_ref, weight_ref = refs[-5:]
    fill_weight(pieces, weight_ref, slice(0, 2 * DV))
    for half in range(TOTAL // SPAN):
        rows = slice(half * SPAN, (half + 1) * SPAN)
        gate_ref[rows, :] = mul(input_ref[rows, :], weight_ref[:, :DV])
    gain = gain_ref[...]
    for part in range(TOTAL // PART):
        out = out_ref[part * PART : (part + 1) * PART, :]
        inv = lax.rsqrt(jnp.mean(out * out, axis=1, keepdims=True) + 1e-06)
        held = part_rows(order_ref, part)
        gate = gate_ref[held, :]
        gated_ref[held, :] = low(out * inv * gain * (gate * sigmoid(gate)))
    for half, mixed_ref in enumerate((keep_ref, send_ref)):
        rows = slice(half * SPAN, (half + 1) * SPAN)
        mixed_ref[...] = low(mul_nt(gated_ref[rows, :], weight_ref[:, DV:]))


def write_grads(pieces, pairs):
    count = len(pieces) - 1
    middle = count // 2
    total = pairs[0][0].shape[1]
    share = total // count
    for block in range(total // SPAN):
        here = slice(block * SPAN, (block + 1) * SPAN)
        at = 0
        for left_ref, right_ref in pairs:
            width = right_ref.shape[1]
            part = low(mul_tn(left_ref[:, here], right_ref[...]))
            for step in range(SPAN // share):
                d = block * (SPAN // share) + step
                rows = part[step * share : (step + 1) * share]
                if d == middle and pieces[d] is None:
                    continue
                if d == middle:
                    pieces[d][:, at : at + width] = rows[: share // 2]
                    pieces[d + 1][:, at : at + width] = rows[share // 2 :]
                else:
                    pieces[d + (d > middle)][:, at : at + width] = rows
            at += width
    for piece in pieces:
        if piece is not None and at < piece.shape[1]:
            piece[:, at:] = jnp.zeros((piece.shape[0], piece.shape[1] - at), BF16)


def ffn_kernel(grad_ref, first_ref, second_ref, third_ref, fourth_ref, *refs):
    pieces = refs[:-10]
    (
        input_ref,
        out_keep_ref,
        out_send_ref,
        back_keep_ref,
        back_send_ref,
        product_ref,
        grads_ref,
        up_ref,
        down_ref,
        weight_ref,
    ) = refs[-10:]
    hidden = product_ref.shape[1]
    own = first_ref.shape[0]
    for at, part in enumerate((first_ref, second_ref, third_ref, fourth_ref)):
        input_ref[at * own : (at + 1) * own, :] = part[...]
    fill_weight(pieces, weight_ref, slice(0, 3 * hidden))
    for half in range(TOTAL // SPAN):
        rows = slice(half * SPAN, (half + 1) * SPAN)
        acts = mul(input_ref[rows, :], weight_ref[:, : 2 * hidden])
        gate = acts[:, :hidden]
        up = acts[:, hidden:]
        sig = sigmoid(gate)
        swish = gate * sig
        product = low(swish * up)
        product_ref[rows, :] = product
        down = weight_ref[:, 2 * hidden :]
        (out_keep_ref, out_send_ref)[half][...] = low(mul_nt(product, down))
        dproduct = mul(grad_ref[rows, :], down)
        dgate = dproduct * up * sig * (1.0 + gate * (1.0 - sig))
        grads_ref[rows, :] = low(jnp.concatenate([dgate, dproduct * swish], axis=1))
        (back_keep_ref, back_send_ref)[half][...] = low(
            mul_nt(grads_ref[rows, :], weight_ref[:, : 2 * hidden])
        )
    width = input_ref.shape[1]
    here = slice(width // 2, width // 2 + width // PIECES)
    cut = up_ref.shape[0]
    at = 0
    for left_ref, right_ref in ((input_ref, grads_ref), (grad_ref, product_ref)):
        cols = slice(at, at + right_ref.shape[1])
        part = low(mul_tn(left_ref[:, here], right_ref[...]))
        up_ref[:, cols] = part[:cut]
        down_ref[:, cols] = part[cut:]
        at += right_ref.shape[1]
    for half_ref in (up_ref, down_ref):
        half_ref[:, at:] = jnp.zeros((cut, half_ref.shape[1] - at), BF16)


def ffn_grads_kernel(input_ref, grads_ref, outer_ref, product_ref, *pieces):
    pieces = [*pieces[:MIDDLE], None, None, *pieces[MIDDLE:]]
    write_grads(pieces, [(input_ref, grads_ref), (outer_ref, product_ref)])


def entry_grads_kernel(input_ref, grads_ref, *pieces):
    write_grads(pieces, [(input_ref, grads_ref)])


def input_back_kernel(
    ahead_ref,
    dproj_ref,
    dgate_ref,
    draw_ref,
    small_ref,
    first_ref,
    second_ref,
    third_ref,
    fourth_ref,
    *refs,
):
    count = (len(refs) - 6) // 2
    keep_ref, send_ref, gain_ref, wide_ref, entry_ref, gate_ref = refs[2 * count :]
    fill_weight(refs[:count], entry_ref, slice(0, FRONT))
    fill_weight(refs[count : 2 * count], gate_ref, slice(0, DV))
    size = wide_ref.shape[0]
    gain = jnp.zeros(gain_ref.shape, F32)
    tokens = (first_ref, second_ref, third_ref, fourth_ref)
    for half, out_ref in enumerate((keep_ref, send_ref)):
        rows = slice(half * SPAN, (half + 1) * SPAN)
        back = mul_nt(dproj_ref[rows, :], entry_ref[...]) + mul_nt(dgate_ref[rows, :], gate_ref[...])
        back = back + mul(draw_ref[rows, :], small_ref[...])
        out_ref[...] = low(back)
        for step in range(SPAN // size):
            ahead_copy(ahead_ref, tokens[half * (SPAN // size) + step], wide_ref, slice(None))
            token = wide_ref[...].astype(F32)
            inv = lax.rsqrt(jnp.mean(token * token, axis=1, keepdims=True) + 1e-06)
            grad = back[step * size : (step + 1) * size]
            gain = gain + jnp.sum(grad * token * inv, axis=0, keepdims=True)
    gain_ref[...] = gain


def summed(keep_ref, near_ref, far_ref):
    own = far_ref.shape[0]
    total = keep_ref[:own, :].astype(F32) + near_ref[:own, :].astype(F32)
    return total + far_ref[...].astype(F32)


def middle_kernel(ahead_ref, tokens_ref, keep_ref, near_ref, far_ref, gain_ref, middle_ref, input_ref, wide_ref):
    ahead_copy(ahead_ref, tokens_ref, wide_ref, slice(None))
    middle = wide_ref[...].astype(F32) + summed(keep_ref, near_ref, far_ref)
    middle_ref[...] = middle
    input_ref[...] = norm_of(middle, gain_ref[...])


def norm_back(rows, grad, gain):
    inv = lax.rsqrt(jnp.mean(rows * rows, axis=1, keepdims=True) + 1e-06)
    pulled = grad * gain
    back = inv * pulled - rows * (inv * inv * inv * jnp.mean(pulled * rows, axis=1, keepdims=True))
    return back, jnp.sum(grad * rows * inv, axis=0, keepdims=True)


def middle_back_kernel(
    ahead_ref, cotangent_ref, middle_ref, keep_ref, near_ref, far_ref, gain_ref, back_ref, low_ref, dgain_ref, wide_ref
):
    ahead_copy(ahead_ref, cotangent_ref, wide_ref, slice(None))
    grad = summed(keep_ref, near_ref, far_ref)
    back, dgain = norm_back(middle_ref[...], grad, gain_ref[...])
    back = wide_ref[...].astype(F32) + back
    back_ref[...] = back
    low_ref[...] = low(back)
    dgain_ref[...] = dgain


def mesh_copy(ahead_ref, source, target_ref):
    count = ahead_ref.shape[0]
    share = target_ref.shape[1] // count
    for d in range(count):
        cols = pl.ds(pl.multiple_of(ahead_ref[d] * share, share), share)
        target_ref[:, cols] = source[:, d * share : (d + 1) * share]


def tokens_back_kernel(ahead_ref, tokens_ref, middle_ref, keep_ref, near_ref, far_ref, gain_ref, out_ref, wide_ref):
    ahead_copy(ahead_ref, tokens_ref, wide_ref, slice(None))
    grad = summed(keep_ref, near_ref, far_ref)
    back, _ = norm_back(wide_ref[...].astype(F32), grad, gain_ref[...])
    mesh_copy(ahead_ref, middle_ref[...] + back, out_ref)


def block_out_kernel(ahead_ref, middle_ref, keep_ref, near_ref, far_ref, out_ref):
    mesh_copy(ahead_ref, low(middle_ref[...] + summed(keep_ref, near_ref, far_ref)), out_ref)


def gate_back_kernel(
    lengths_ref,
    order_ref,
    first_ref,
    second_ref,
    third_ref,
    fourth_ref,
    gate_ref,
    gain_ref,
    out_ref,
    input_ref,
    gated_ref,
    *refs,
):
    weights, refs = refs[: PIECES + 1], refs[PIECES + 1 :]
    dgate_ref, dout_ref, dgain_ref = refs[:3]
    grad_ref, mixed_ref, weight_ref = refs[-3:]
    own = first_ref.shape[0]
    for at, part in enumerate((first_ref, second_ref, third_ref, fourth_ref)):
        mixed_ref[at * own : (at + 1) * own, :] = part[...]
    fill_weight(weights, weight_ref, slice(DV, 2 * DV))
    for half in range(TOTAL // SPAN):
        rows = slice(half * SPAN, (half + 1) * SPAN)
        grad_ref[rows, :] = mul(mixed_ref[rows, :], weight_ref[...])
    start = second_start(lengths_ref)
    gain = gain_ref[...]
    dgain = jnp.zeros((1, DV), F32)
    for part in range(TOTAL // PART):
        here = slice(part * PART, (part + 1) * PART)
        held = part_rows(order_ref, part)
        out = out_ref[here, :]
        gate = gate_ref[held, :]
        grad = grad_ref[held, :]
        inv = lax.rsqrt(jnp.mean(out * out, axis=1, keepdims=True) + 1e-06)
        sig = sigmoid(gate)
        swish = gate * sig
        unit = out * inv
        pulled = grad * unit
        dgate_ref[held, :] = low(pulled * gain * (sig * (1.0 + gate * (1.0 - sig))))
        dgain = dgain + jnp.sum(pulled * swish, axis=0, keepdims=True)
        inner = grad * swish * gain
        dout = inv * (inner - unit * jnp.mean(inner * unit, axis=1, keepdims=True))
        dout = jnp.where(row_limit(lengths_ref, start, part * PART, PART), dout, 0.0)
        keep_halves(dout_ref, here, halves(dout))
    dgain_ref[...] = dgain
    write_grads(refs[3:-3], [(input_ref, dgate_ref), (mixed_ref, gated_ref)])


def back_kernel(
    lengths_ref,
    order_ref,
    rates_ref,
    proj_ref,
    taps_ref,
    dout_ref,
    raw_ref,
    query_ref,
    key_ref,
    value_ref,
    state_ref,
    inverse_ref,
    reach_ref,
    fresh_ref,
    dproj_ref,
    draw_ref,
    dtaps_ref,
    drates_ref,
    dfresh_ref,
    dstate_ref,
    carry_ref,
    dq_ref,
    dk_ref,
    dv_ref,
    halo_ref,
):
    start = second_start(lengths_ref)
    rate = rates_ref[0, 0]
    bias = rates_ref[1, 0]
    masks = span_masks()
    rows, cols, same = masks
    causal = same & (rows >= cols)
    strict = same & (rows > cols)

    kept = []
    for span in range(SPANS):
        at = slice(span * SPAN, (span + 1) * SPAN)
        dout = read_halves(dout_ref, at)
        raw = raw_ref[at, :]
        beta = sigmoid(raw[:, 0:1])
        column, running, final, ratio = decay_terms(raw[:, 1:2], rate, bias, masks)
        growth = jnp.exp(running)
        tail = jnp.exp(final - running)
        key = key_ref[at, :]
        score = mul_nt(query_ref[at, :], key) * ratio
        dfresh_ref[at, :] = fine(mul_tn, halves(score), dout)
        dscore = jnp.where(causal, fine(mul_nt, dout, read_halves(fresh_ref, at)), 0.0)
        tailed = halves(tail * key.astype(F32))
        kept.append((beta, column, growth, final, tail, ratio, score, dscore, tailed))

    carry_ref[...] = jnp.zeros_like(carry_ref)
    ends = [None] * BLOCKS
    for index in reversed(range(BLOCKS)):
        at = slice(index * BLOCK, (index + 1) * BLOCK)
        low_at = index * BLOCK % SPAN
        inner = slice(low_at, low_at + BLOCK)
        beta, column, growth, final, tail, ratio, score, dscore, tailed = kept[index * BLOCK // SPAN]
        held = carry_ref[...]
        dstate = low(held)
        dstate_ref[index] = dstate
        both = mul(rows_of(tailed[0][inner], tailed[1][inner]), dstate)
        dfresh = dfresh_ref[at, :] + both[:BLOCK] + both[BLOCK:]
        dfresh_ref[at, :] = dfresh
        scale = jnp.exp(final[low_at : low_at + 1])
        if index > 0:
            read = halves(query_ref[at, :].astype(F32) * growth[inner])
            reach = read_halves(reach_ref, at)
            dout = read_halves(dout_ref, at)
            dfresh = halves(dfresh)
            gained = mul_tn(rows_of(*read, read[0]), rows_of(dout[0], dout[0], dout[1]))
            lost = mul_tn(rows_of(*reach, reach[0]), rows_of(dfresh[0], dfresh[0], dfresh[1]))
            carry_ref[...] = jnp.where(
                start == index * BLOCK, 0.0, scale * held + gained - lost
            )
        ends[index] = scale * jnp.sum(
            jnp.sum(held * state_ref[index].astype(F32), axis=0, keepdims=True), axis=1, keepdims=True
        )

    drate = jnp.zeros((1, 1), F32)
    dbias = jnp.zeros((1, 1), F32)
    steps = SPAN // BLOCK
    for span in range(SPANS):
        at = slice(span * SPAN, (span + 1) * SPAN)
        beta, column, growth, final, tail, ratio, score, dscore, tailed = kept[span]
        query = query_ref[at, :]
        key = key_ref[at, :]
        key_wide = key.astype(F32)
        dright = fine(mul_tn, read_halves(inverse_ref, at), halves(dfresh_ref[at, :]))
        dright_halves = halves(dright)
        dcouple = jnp.where(strict, -fine(mul_nt, dright_halves, read_halves(fresh_ref, at)), 0.0)
        cross = mul_nt(key, key) * ratio
        weighted = dcouple * cross
        dbeta = jnp.sum(weighted, axis=1, keepdims=True)
        ratio_grad = dscore * score + weighted * beta
        dintersect = low(dcouple * beta * ratio)
        dscored = low(dscore * ratio)
        dquery = mul(dscored, key)
        dkey = mul_tn(dscored, query) + mul(dintersect, key) + mul_tn(dintersect, key)
        pieces = [[], [], []]
        for step in range(steps):
            index = span * steps + step
            here = slice(index * BLOCK, (index + 1) * BLOCK)
            inner = slice(step * BLOCK, (step + 1) * BLOCK)
            joined = rows_of(*read_halves(dout_ref, here), *[one[inner] for one in dright_halves])
            back = mul_nt(joined, state_ref[index])
            pieces[0].append(back[:BLOCK] + back[BLOCK : 2 * BLOCK])
            pieces[1].append(back[2 * BLOCK : 3 * BLOCK] + back[3 * BLOCK :])
            back = mul_nt(rows_of(*read_halves(fresh_ref, here)), dstate_ref[index])
            pieces[2].append(back[:BLOCK] + back[BLOCK:])
        out_back, right_back, tail_back = [jnp.concatenate(piece, axis=0) for piece in pieces]
        dquery = dquery + growth * out_back
        read = jnp.sum(key_wide * right_back, axis=1, keepdims=True)
        dkey = dkey - (beta * growth) * right_back + tail * tail_back
        dbeta = (
            dbeta
            + jnp.sum(dright * value_ref[at, :].astype(F32), axis=1, keepdims=True)
            - growth * read
        )
        dgrowth = jnp.sum(query.astype(F32) * out_back, axis=1, keepdims=True) - beta * read
        dtail = tail * jnp.sum(key_wide * tail_back, axis=1, keepdims=True)
        flat = jnp.sum(
            jnp.where(rows == cols, jnp.sum(ratio_grad, axis=0, keepdims=True), 0.0),
            axis=1,
            keepdims=True,
        )
        drunning = growth * dgrowth + jnp.sum(ratio_grad, axis=1, keepdims=True) - flat - dtail
        line = jnp.sum(jnp.where(rows == cols, drunning, 0.0), axis=0, keepdims=True)
        tail_line = jnp.sum(jnp.where(rows == cols, dtail, 0.0), axis=0, keepdims=True)
        ending = jnp.concatenate(
            [jnp.broadcast_to(ends[span * steps + step], (BLOCK, 1)) for step in range(steps)],
            axis=0,
        )
        dlog = (
            jnp.sum(jnp.where(same & (rows <= cols), line, 0.0), axis=1, keepdims=True)
            + jnp.sum(jnp.where(same, tail_line, 0.0), axis=1, keepdims=True)
            + ending
        )
        raw = raw_ref[at, :]
        ddecay = -jnp.exp(rate) * dlog * sigmoid(raw[:, 1:2] + bias)
        drate = drate + jnp.sum(dlog * column, axis=0, keepdims=True)
        dbias = dbias + jnp.sum(ddecay, axis=0, keepdims=True)
        dbeta = dbeta * beta * (1.0 - beta)
        lane = lax.broadcasted_iota(jnp.int32, (SPAN, PACK), 1)
        draw = low(jnp.where(lane == 0, dbeta, jnp.where(lane == 1, ddecay, 0.0)))
        for half in range(SPAN // PART):
            held = part_rows(order_ref, span * (SPAN // PART) + half)
            draw_ref[held, :] = draw[half * PART : (half + 1) * PART]
        dq_ref[at, :] = low(dquery)
        dk_ref[at, :] = low(dkey)
        dv_ref[at, :] = low(beta * dright)
    lane = lax.broadcasted_iota(jnp.int32, (8, 128), 1)
    drates_ref[...] = jnp.where(lane == 0, drate, jnp.where(lane == 1, dbias, 0.0))

    dtaps_ref[...] = jnp.zeros_like(dtaps_ref)
    halo_ref[...] = jnp.zeros_like(halo_ref)

    def back(step, carry):
        index = BLOCKS - 1 - step
        base = pl.multiple_of(index * BLOCK, BLOCK)
        held = held_rows(order_ref, index)
        before = past_rows(order_ref, index)
        broken = (base == 0) | (base == start)
        ended = (base + BLOCK == TOTAL) | (base + BLOCK == start)
        for at in range(0, FRONT, DK):
            here = slice(at, at + DK)
            taps = taps_ref[:, here]
            halo = jnp.where(broken, 0.0, proj_ref[pl.ds(before, 8), here])
            block = proj_ref[pl.ds(held, BLOCK), here]
            joined = jnp.concatenate([halo, block], axis=0)
            shifted = [block] + [pltpu.roll(joined, offset, 0)[8:] for offset in range(1, 4)]
            conv = shifted[0] * taps[0:1]
            for offset in range(1, 4):
                conv = conv + shifted[offset] * taps[offset : offset + 1]
            sig = sigmoid(conv)
            if at >= 2 * DK:
                dact = dv_ref[pl.ds(base, BLOCK), at - 2 * DK : at - DK].astype(F32)
            else:
                act = conv * sig
                given = (dq_ref if at == 0 else dk_ref)[pl.ds(base, BLOCK), :].astype(F32)
                inv = lax.rsqrt(jnp.sum(act * act, axis=1, keepdims=True) + 1e-06)
                along = jnp.sum(act * given, axis=1, keepdims=True)
                dact = inv * (given - act * (inv * inv * along))
                if at == 0:
                    dact = dact * DK ** (-0.5)
            dconv = dact * (sig * (1.0 + conv * (1.0 - sig)))
            after = jnp.where(ended, 0.0, halo_ref[:, here])
            halo_ref[:, here] = dconv[:8]
            trailing = jnp.concatenate([dconv, after], axis=0)
            dblock = dconv * taps[0:1]
            for offset in range(1, 4):
                moved = pltpu.roll(trailing, BLOCK + 8 - offset, 0)[:BLOCK]
                dblock = dblock + moved * taps[offset : offset + 1]
            dproj_ref[pl.ds(held, BLOCK), here] = low(dblock)
            for offset in range(4):
                dtaps_ref[offset : offset + 1, here] += jnp.sum(
                    dconv * shifted[offset], axis=0, keepdims=True
                )
        return carry

    lax.fori_loop(0, BLOCKS, back, 0)


def entry_kernel(
    query_ref,
    key_ref,
    value_ref,
    beta_ref,
    decay_ref,
    norm_ref,
    ffn_ref,
    query_conv_ref,
    key_conv_ref,
    value_conv_ref,
    gain_ref,
    out_ref,
    small_ref,
):
    rows = query_ref.shape[0]
    wide = query_ref.shape[1]
    out_ref[:rows, :wide] = query_ref[...]
    out_ref[:rows, wide : 2 * wide] = key_ref[...]
    out_ref[:rows, 2 * wide :] = value_ref[...]
    small_ref[...] = jnp.zeros_like(small_ref)
    for at, line in enumerate((beta_ref, decay_ref, norm_ref, ffn_ref)):
        small_ref[at : at + 1, :] = line[...].astype(F32)
    taps = query_conv_ref.shape[0]
    cols = 0
    for conv in (query_conv_ref, key_conv_ref, value_conv_ref):
        small_ref[4 : 4 + taps, cols : cols + conv.shape[1]] = conv[...].astype(F32)
        cols += conv.shape[1]
    small_ref[8:9, : gain_ref.shape[1]] = gain_ref[...].astype(F32)
    out_ref[rows:, :] = jnp.zeros((PACK, out_ref.shape[1]), BF16)
    out_ref[rows:, :rows] = low(small_ref[...])


def pack_kernel(behind_ref, *refs):
    packs = refs[:PIECES]
    norm_ref, ffn_ref, small_ref, taps_ref, gain_ref, all_ref = refs[PIECES:]
    share = packs[0].shape[1]
    for d, pack in enumerate(packs):
        here = slice(d * share, (d + 1) * share)
        small_ref[:, here] = pack[...]
        wide = pack[...].astype(F32)
        all_ref[d] = wide
        norm_ref[:, here] = wide[2:3]
        ffn_ref[:, here] = wide[3:4]
    narrow = DK // PIECES
    for n in range(PIECES):
        wide = all_ref[behind_ref[n]]
        taps_ref[:, n * narrow : (n + 1) * narrow] = wide[4:8, :narrow]
        taps_ref[:, DK + n * narrow : DK + (n + 1) * narrow] = wide[4:8, narrow : 2 * narrow]
        at = 2 * DK + n * 2 * narrow
        taps_ref[:, at : at + 2 * narrow] = wide[4:8, 2 * narrow :]
        gain_ref[:, n * 2 * narrow : (n + 1) * 2 * narrow] = wide[8:9, : 2 * narrow]


def pack_call(behind, pieces, share, width):
    rows = [share // PACK] * (PIECES + 1)
    rows[MIDDLE + 1] = share // 2 // PACK
    picked = [d for d in range(PIECES + 1) if d != MIDDLE]

    def block(at):
        return pl.BlockSpec((PACK, share), lambda i: (at, 0))

    line = jax.ShapeDtypeStruct((1, width), F32)
    whole = lambda shape: pl.BlockSpec(shape, lambda i: (0, 0))
    shapes = (
        line,
        line,
        jax.ShapeDtypeStruct((PACK, width), BF16),
        jax.ShapeDtypeStruct((4, FRONT), F32),
        jax.ShapeDtypeStruct((1, DV), F32),
    )
    return pl.pallas_call(
        pack_kernel,
        grid=(1,),
        out_shape=shapes,
        in_specs=[pl.BlockSpec(memory_space=SMEM)] + [block(rows[d]) for d in picked],
        out_specs=tuple(whole(one.shape) for one in shapes),
        scratch_shapes=[pltpu.VMEM((PIECES, PACK, share), F32)],
        name="pack",
    )(behind, *[pieces[d] for d in picked])


def run_kernel(kernel, name, scalars, arrays, results, scratch, cost):
    return pl.pallas_call(
        kernel,
        out_shape=tuple(jax.ShapeDtypeStruct(shape, kind) for shape, kind in results),
        in_specs=[pl.BlockSpec(memory_space=SMEM)] * len(scalars)
        + [pl.BlockSpec(memory_space=VMEM)] * len(arrays),
        out_specs=tuple([pl.BlockSpec(memory_space=VMEM)] * len(results)),
        scratch_shapes=[pltpu.VMEM(shape, kind) for shape, kind in scratch],
        compiler_params=pltpu.CompilerParams(vmem_limit_bytes=LIMIT),
        cost_estimate=pl.CostEstimate(
            flops=cost * 1_000_000_000, bytes_accessed=8_000_000, transcendentals=1_000_000
        ),
        name=name,
    )(*scalars, *arrays)


def front_call(lengths, order, rates, taps, rows, small, pieces):
    results = (
        ((TOTAL, FRONT), F32),
        ((TOTAL, DK), BF16),
        ((TOTAL, DK), BF16),
        ((TOTAL, DV), BF16),
        ((TOTAL, PACK), F32),
        ((TOTAL, 2 * SPAN), BF16),
        ((TOTAL, 2 * DK), BF16),
        ((TOTAL, DV), F32),
        ((TOTAL, 2 * DK), BF16),
        ((TOTAL, 2 * SPAN), BF16),
        ((TOTAL, 128), F32),
    )
    return run_kernel(
        front_kernel,
        "mixer_front",
        (lengths, order, rates),
        (taps, rows, small, *pieces),
        results,
        (((rows.shape[1], FRONT), BF16),),
        15,
    )


def chain_call(lengths, arrays):
    results = (((BLOCKS, DK, DV), BF16), ((TOTAL, 2 * DV), BF16), ((TOTAL, DV), F32))
    return run_kernel(
        chain_kernel, "mixer_chain", (lengths,), arrays, results, (((DK, DV), F32),), 7
    )


def gate_call(order, arrays, width):
    half = ((SPAN, width), BF16)
    results = (((TOTAL, DV), F32), ((TOTAL, DV), BF16), half, half)
    return run_kernel(
        gate_kernel, "mixer_gate", (order,), arrays, results, (((width, 2 * DV), BF16),), 6
    )


def gate_back_call(lengths, order, arrays, shapes, width):
    scratch = (((TOTAL, DV), F32), ((TOTAL, width), BF16), ((width, DV), BF16))
    results = (((TOTAL, DV), BF16), ((TOTAL, 2 * DV), BF16), ((1, DV), F32), *shapes)
    return run_kernel(
        gate_back_kernel, "gate_back", (lengths, order), arrays, results, scratch, 7
    )


def back_call(lengths, order, rates, arrays):
    results = (
        ((TOTAL, FRONT), BF16),
        ((TOTAL, PACK), BF16),
        ((4, FRONT), F32),
        ((8, 128), F32),
    )
    scratch = (
        ((TOTAL, DV), F32),
        ((BLOCKS, DK, DV), BF16),
        ((DK, DV), F32),
        ((TOTAL, DK), BF16),
        ((TOTAL, DK), BF16),
        ((TOTAL, DV), BF16),
        ((8, FRONT), F32),
    )
    return run_kernel(
        back_kernel, "mixer_back", (lengths, order, rates), arrays, results, scratch, 17
    )


def plain_product(left, right):
    return jnp.dot(left, right, preferred_element_type=F32)


def transposed_product(left, right):
    return lax.dot_general(left, right, (((0,), (0,)), ((), ())), preferred_element_type=F32)


def product_back(grad, weight):
    return lax.dot_general(grad, weight, (((1,), (1,)), ((), ())), preferred_element_type=F32)


def piece_shapes(width, share):
    full = ((share, width), BF16)
    half = ((share // 2, width), BF16)
    return [half if d in (MIDDLE, MIDDLE + 1) else full for d in range(PIECES + 1)]


def cut_rows(whole):
    share = whole.shape[0] // PIECES
    middle = MIDDLE * share
    cuts = [d * share for d in range(MIDDLE + 1)] + [middle + share // 2]
    cuts += [d * share for d in range(MIDDLE + 1, PIECES + 1)]
    return [whole[a:b] for a, b in zip(cuts[:-1], cuts[1:])]


class Ring:
    def __init__(self, count):
        self.count = count
        self.circle = count == PIECES
        if self.circle:
            self.order = list(range(0, count, 2)) + list(range(count - 1, 0, -2))
            place = [self.order.index(i) for i in range(count)]
            ahead = [[self.order[(place[i] + d) % count] for d in range(count)] for i in range(count)]
            behind = [[(place[j] - place[i]) % count for j in range(count)] for i in range(count)]
            here = lax.axis_index("dp")
            self.ahead = jnp.array(ahead, jnp.int32)[here]
            self.behind = jnp.array(behind, jnp.int32)[here]
        else:
            self.ahead = jnp.arange(PIECES, dtype=jnp.int32)

    def step(self, value, places):
        pairs = [
            (self.order[i], self.order[(i + places) % self.count]) for i in range(self.count)
        ]
        return lax.ppermute(value, "dp", pairs)

    def halved(self, value, distance):
        if not self.circle:
            return value
        width = value.shape[1] // 2
        side = lax.axis_index("dp") // distance % 2
        kept = lax.dynamic_slice_in_dim(value, side * width, width, axis=1)
        sent = lax.dynamic_slice_in_dim(value, (1 - side) * width, width, axis=1)
        pairs = [(i, i ^ distance) for i in range(self.count)]
        return kept + lax.ppermute(sent, "dp", pairs)


class Gather:
    def __init__(self, ring, part, share):
        self.ring, self.part, self.share = ring, part, share
        self.flight = (part, part)
        self.steps = []
        if not ring.circle:
            self.whole = lax.all_gather(part, "dp", axis=0)

    def hop(self):
        if not self.ring.circle:
            return
        up, down = self.flight
        if len(self.steps) == MIDDLE - 1:
            up, down = up[: self.share // 2], down[self.share // 2 :]
        self.flight = (self.ring.step(up, 1), self.ring.step(down, -1))
        self.steps.append(self.flight)

    def held(self):
        return self.flight if self.ring.circle else ()

    def take(self, flight):
        if self.ring.circle:
            self.flight = flight
            self.steps[-1] = flight

    def pieces(self):
        if not self.ring.circle:
            return cut_rows(self.whole[:, : self.share].reshape(-1, self.whole.shape[2]))
        *full, last = self.steps
        return [self.part, *[down for _, down in full], *last, *[up for up, _ in reversed(full)]]

    def packs(self):
        if not self.ring.circle:
            return self.whole[:, self.share :, : self.share]
        rows = self.pieces()
        half = self.share // 2
        packs = [piece[self.share :, : self.share] for piece in rows]
        packs[MIDDLE + 1] = rows[MIDDLE + 1][half:, : self.share]
        return jnp.stack(packs[:MIDDLE] + packs[MIDDLE + 1 :])


class Scatter:
    def __init__(self, ring, up, down):
        self.ring, self.first = ring, (up, down)
        self.flight = ()
        self.left = MIDDLE

    def rest(self, pieces):
        self.pieces = [*pieces[:MIDDLE], *self.first, *pieces[MIDDLE:]]
        if not self.ring.circle:
            whole = jnp.concatenate(self.pieces, axis=0)
            self.whole = lax.psum_scatter(whole, "dp", scatter_dimension=0, tiled=True)

    def hop(self):
        if not self.ring.circle:
            return
        if self.left == MIDDLE:
            up, down = self.first
        else:
            pieces = self.pieces
            ahead = pieces[self.left].astype(F32)
            back = pieces[len(pieces) - self.left].astype(F32)
            up, down = [one.astype(F32) for one in self.flight]
            cut = up.shape[0]
            if self.left == MIDDLE - 1:
                up = jnp.concatenate([ahead[:cut] + up, ahead[cut:]], axis=0)
                down = jnp.concatenate([back[:cut], back[cut:] + down], axis=0)
            else:
                up = ahead + up
                down = back + down
            up, down = low(up), low(down)
        self.flight = (self.ring.step(up, 1), self.ring.step(down, -1))
        self.left -= 1

    def held(self):
        return self.flight

    def take(self, flight):
        self.flight = flight


def finish_kernel(first_ref, up_ref, down_ref, *outs):
    total = first_ref[...].astype(F32) + up_ref[...].astype(F32) + down_ref[...].astype(F32)
    rows = first_ref.shape[0]
    at = 0
    for out in outs:
        turned = out.shape[0] != rows
        width = out.shape[0] if turned else out.shape[1]
        piece = total[:, at : at + width]
        out[...] = piece.T if turned else piece
        at += width


def finish(sums, shapes):
    if not sums.ring.circle:
        total = sums.whole.astype(F32)
        outs, at = [], 0
        for shape in shapes:
            turned = shape[0] != total.shape[0]
            width = shape[0] if turned else shape[1]
            piece = total[:, at : at + width]
            outs.append(piece.T if turned else piece)
            at += width
        return outs
    return run_kernel(
        finish_kernel,
        "finish",
        (),
        (sums.pieces[0], *sums.flight),
        [(shape, F32) for shape in shapes],
        (),
        2,
    )


def sync(moving, *values):
    flights, values = lax.optimization_barrier(([one.held() for one in moving], values))
    for one, flight in zip(moving, flights):
        one.take(flight)
    return values


def swap(value, distance):
    count = lax.axis_size("tensor")
    return lax.ppermute(value, "tensor", [(i, i ^ distance) for i in range(count)])


def folded(keep, near):
    own = keep.shape[0] // 2
    return low(keep[own:].astype(F32) + near[own:].astype(F32))


def local(
    tokens,
    lengths,
    cotangent,
    norm_gain,
    query_weight,
    key_weight,
    value_weight,
    gate_weight,
    beta_weight,
    decay_weight,
    query_conv,
    key_conv,
    value_conv,
    decay_params,
    head_gain,
    out_weight,
    ffn_gain,
    ffn_gate,
    ffn_up,
    ffn_down,
):
    count = lax.axis_size("dp")
    team = lax.axis_size("tensor")
    ring = Ring(count)
    ahead = ring.ahead
    place = lax.axis_index("tensor")
    swapped = [[[0, 2, 1, 3][i ^ t] for i in range(team)] for t in range(team)]
    order = jnp.array(swapped, jnp.int32)[place]
    share = norm_gain.shape[0]
    narrow = head_gain.shape[0]
    narrow_q = query_conv.shape[1]
    cuts = (0, narrow_q, 2 * narrow_q, share)
    width = tokens.shape[1]
    hidden = ffn_gate.shape[1]
    own = tokens.shape[0]
    low_rows = ((own, width), BF16)
    wide_rows = ((own, width), F32)
    wide_line = ((1, width), F32)

    padded = -(-3 * hidden // 128) * 128
    half_rows = ((SPAN, width), BF16)
    entry = pl.pallas_call(
        entry_kernel,
        out_shape=jax.ShapeDtypeStruct((share + PACK, FRONT), BF16),
        scratch_shapes=[pltpu.VMEM((PACK, share), F32)],
        name="entry",
    )(
        query_weight,
        key_weight,
        value_weight,
        beta_weight.reshape(1, share),
        decay_weight.reshape(1, share),
        norm_gain.reshape(1, share),
        ffn_gain.reshape(1, share),
        query_conv,
        key_conv,
        value_conv,
        head_gain.reshape(1, narrow),
    )
    entries = Gather(ring, entry, share)
    entries.hop()
    tokens_2, tokens_1, cotangent, out_weight, gate_weight, ffn_gate, ffn_up, ffn_down = sync(
        [entries],
        swap(tokens, 2),
        swap(tokens, 1),
        cotangent,
        out_weight,
        gate_weight,
        ffn_gate,
        ffn_up,
        ffn_down,
    )
    entries.hop()
    tokens_3, grads_2, grads_1, side, ffn_gate, ffn_up, ffn_down = sync(
        [entries],
        swap(tokens_2, 1),
        swap(cotangent, 2),
        swap(cotangent, 1),
        jnp.concatenate([gate_weight, out_weight.T], axis=1),
        ffn_gate,
        ffn_up,
        ffn_down,
    )
    entries.hop()
    blank = jnp.zeros((share, padded - 3 * hidden), BF16)
    grads_3, side, wide = sync(
        [entries],
        swap(grads_2, 1),
        side,
        jnp.concatenate([ffn_gate, ffn_up, ffn_down.T, blank], axis=1),
    )
    sides = Gather(ring, side, share)
    entries.hop()
    sides.hop()
    (wide,) = sync([entries, sides], wide)

    sides.hop()
    entry_pieces = entries.pieces()
    if ring.circle:
        norm_whole, ffn_gain_whole, small, taps, gains = pack_call(
            ring.behind, entry_pieces, share, width
        )
    else:
        packs = jnp.swapaxes(entries.packs(), 0, 1)
        norm_whole = packs[2].reshape(1, width).astype(F32)
        ffn_gain_whole = packs[3].reshape(1, width).astype(F32)
        small = packs.reshape(PACK, width)
        packs = packs[4:9].astype(F32)
        taps = jnp.concatenate(
            [packs[:4, :, a:b].reshape(4, -1) for a, b in zip(cuts[:-1], cuts[1:])], axis=1
        )
        gains = packs[4, :, :narrow].reshape(1, DV)
    mixer_input, down_grad = run_kernel(
        gather_kernel,
        "gather",
        (ahead,),
        (norm_whole, tokens, tokens_2, tokens_1, tokens_3, cotangent, grads_2, grads_1, grads_3),
        (((TOTAL, width), BF16), ((TOTAL, width), BF16)),
        (low_rows,),
        4,
    )
    mixer_input, down_grad, taps, gains, small, ffn_gain_whole, norm_whole, wide = sync(
        [sides], mixer_input, down_grad, taps, gains, small, ffn_gain_whole, norm_whole, wide
    )

    wides = Gather(ring, wide, share)
    sides.hop()
    wides.hop()
    front = front_call(lengths, order, decay_params, taps, mixer_input, small, entry_pieces)
    proj, query, key, value, raw, inverse, reach, base, tail, score, growth = sync(
        [sides, wides], *front
    )

    sides.hop()
    wides.hop()
    state, fresh, out = sync(
        [sides], *chain_call(lengths, (query, reach, base, tail, score, growth))
    )
    side_pieces = sides.pieces()
    gate, gated, keep, send = sync(
        [wides], *gate_call(order, (out, gains, mixer_input, *side_pieces), width)
    )
    wides.hop()
    near, keep = sync([], swap(send, 1), keep)
    far, keep, near = sync([], swap(folded(keep, near), 2), keep, near)

    middle, second = run_kernel(
        middle_kernel,
        "middle",
        (ahead,),
        (tokens, keep, near, far, ffn_gain_whole),
        (wide_rows, low_rows),
        (low_rows,),
        2,
    )
    middle, second = sync([wides], middle, second)
    wides.hop()
    second_2, second_1 = sync([], swap(second, 2), swap(second, 1))
    (second_3,) = sync([wides], swap(second_2, 1))

    ffn_pieces = wides.pieces()
    ffn_input, out_keep, out_send, keep, send, product, grad_acts, grads_up, grads_down = sync(
        [],
        *run_kernel(
            ffn_kernel,
            "ffn",
            (),
            (down_grad, second, second_2, second_1, second_3, *ffn_pieces),
            (
                ((TOTAL, width), BF16),
                half_rows,
                half_rows,
                half_rows,
                half_rows,
                ((TOTAL, hidden), BF16),
                ((TOTAL, 2 * hidden), BF16),
                *piece_shapes(padded, width // PIECES)[MIDDLE : MIDDLE + 2],
            ),
            (((width, 3 * hidden), BF16),),
            13,
        ),
    )

    ffn_sums = Scatter(ring, grads_up, grads_down)
    ffn_sums.hop()
    shapes = piece_shapes(padded, width // PIECES)
    near, keep, out_keep, out_send, *ffn_grads = sync(
        [ffn_sums],
        swap(send, 1),
        keep,
        out_keep,
        out_send,
        *run_kernel(
            ffn_grads_kernel,
            "ffn_grads",
            (),
            (ffn_input, grad_acts, down_grad, product),
            shapes[:MIDDLE] + shapes[MIDDLE + 2 :],
            (),
            7,
        ),
    )
    ffn_sums.rest(ffn_grads)
    ffn_sums.hop()
    far, keep, near, out_keep, out_near = sync(
        [], swap(folded(keep, near), 2), keep, near, out_keep, swap(out_send, 1)
    )

    grad_middle, grad_mixed, dffn_gain = run_kernel(
        middle_back_kernel,
        "middle_back",
        (ahead,),
        (cotangent, middle, keep, near, far, ffn_gain_whole),
        (wide_rows, low_rows, wide_line),
        (low_rows,),
        3,
    )
    grad_middle, grad_mixed, dffn_gain, mixed_2, mixed_1, out_keep, out_near = sync(
        [ffn_sums],
        grad_middle,
        grad_mixed,
        dffn_gain,
        swap(grad_mixed, 2),
        swap(grad_mixed, 1),
        out_keep,
        out_near,
    )

    ffn_sums.hop()
    dgate, dout, dgain, *side_grads = gate_back_call(
        lengths,
        order,
        (
            grad_mixed,
            mixed_2,
            mixed_1,
            swap(mixed_2, 1),
            gate,
            gains,
            out,
            mixer_input,
            gated,
            *side_pieces,
        ),
        piece_shapes(2 * DV, width // PIECES),
        width,
    )
    dgate, dout, dgain, out_keep, out_near, *side_grads = sync(
        [ffn_sums], dgate, dout, dgain, out_keep, out_near, *side_grads
    )

    ffn_sums.hop()
    side_sums = Scatter(ring, *side_grads[MIDDLE : MIDDLE + 2])
    side_sums.rest(side_grads[:MIDDLE] + side_grads[MIDDLE + 2 :])
    side_sums.hop()
    out_far = swap(folded(out_keep, out_near), 2)
    dproj, draw, dtaps, drates, out_far, out_keep, out_near = sync(
        [ffn_sums, side_sums],
        *back_call(
            lengths,
            order,
            decay_params,
            (proj, taps, dout, raw, query, key, value, state, inverse, reach, fresh),
        ),
        out_far,
        out_keep,
        out_near,
    )

    side_sums.hop()
    keep, send, dnorm = run_kernel(
        input_back_kernel,
        "input_back",
        (ahead,),
        (
            dproj,
            dgate,
            draw,
            small,
            tokens,
            tokens_2,
            tokens_1,
            tokens_3,
            *entry_pieces,
            *side_pieces,
        ),
        (half_rows, half_rows, wide_line),
        (low_rows, ((width, FRONT), BF16), ((width, DV), BF16)),
        6,
    )
    keep, send, dnorm, dffn_gain, dtaps, dgain, drates, out_far, *entry_grads = sync(
        [side_sums, ffn_sums],
        keep,
        send,
        dnorm,
        dffn_gain,
        dtaps,
        dgain,
        drates,
        out_far,
        *run_kernel(
            entry_grads_kernel,
            "entry_grads",
            (),
            (mixer_input, dproj),
            piece_shapes(FRONT, width // PIECES),
            (),
            5,
        ),
    )

    side_sums.hop()
    entry_sums = Scatter(ring, *entry_grads[MIDDLE : MIDDLE + 2])
    entry_sums.rest(entry_grads[:MIDDLE] + entry_grads[MIDDLE + 2 :])
    entry_sums.hop()
    lines = jnp.concatenate([dnorm, dffn_gain], axis=0)
    near, keep, lines, dtaps, dgain, drates, out_far = sync(
        [side_sums, entry_sums, ffn_sums],
        swap(send, 1),
        keep,
        lines + swap(lines, 1),
        dtaps,
        dgain,
        drates,
        out_far,
    )

    side_sums.hop()
    entry_sums.hop()
    channel_grads = jnp.concatenate(
        [
            dtaps[:, a * count : b * count].reshape(4, count, b - a)
            for a, b in zip(cuts[:-1], cuts[1:])
        ],
        axis=2,
    )
    gain_grads = jnp.pad(dgain.reshape(1, count, narrow), ((0, 0), (0, 0), (0, share - narrow)))
    channel_grads = jnp.concatenate([channel_grads, gain_grads], axis=0)
    lines = jnp.concatenate(
        [transposed_product(draw, mixer_input)[:2], lines + swap(lines, 2)], axis=0
    )
    if ring.circle:
        lines = lines.reshape(4, count, share)[:, ring.behind].reshape(4, width)
    pack_grad = jnp.concatenate(
        [
            lines,
            channel_grads.reshape(5, width),
            jnp.broadcast_to(drates[0:1, 0:1], (1, width)),
            jnp.broadcast_to(drates[0:1, 1:2], (1, width)),
            jnp.zeros((PACK - 11, width), F32),
        ],
        axis=0,
    )
    far, keep, near, pack_grad, out_far = sync(
        [side_sums, entry_sums, ffn_sums],
        swap(folded(keep, near), 2),
        keep,
        near,
        pack_grad,
        out_far,
    )

    entry_sums.hop()
    ffn_outs = finish(ffn_sums, ((hidden, share), (hidden, share), (hidden, share)))
    tokens_grad, dgate_weight, dup_weight, ddown_weight, out_far, pack_grad = sync(
        [side_sums, entry_sums],
        run_kernel(
            tokens_back_kernel,
            "tokens_back",
            (ahead,),
            (tokens, grad_middle, keep, near, far, norm_whole),
            (wide_rows,),
            (low_rows,),
            3,
        )[0],
        *ffn_outs,
        out_far,
        ring.halved(pack_grad, 4),
    )

    entry_sums.hop()
    side_outs = finish(side_sums, ((share, DV), (DV, share)))
    block_out, dside_weight, dout_weight, pack_sum = sync(
        [entry_sums],
        run_kernel(
            block_out_kernel,
            "block_out",
            (ahead,),
            (middle, out_keep, out_near, out_far),
            (low_rows,),
            (),
            3,
        )[0],
        *side_outs,
        ring.halved(pack_grad, 2),
    )

    pack_sum = ring.halved(pack_sum, 1)
    if not ring.circle:
        pack_sum = lax.psum_scatter(pack_sum, "dp", scatter_dimension=1, tiled=True)
    query_out, key_out, value_out = finish(entry_sums, ((share, DK), (share, DK), (share, DV)))
    return (
        block_out,
        tokens_grad,
        pack_sum[2],
        query_out,
        key_out,
        value_out,
        dside_weight,
        pack_sum[0][:, None],
        pack_sum[1][:, None],
        pack_sum[4:8, cuts[0] : cuts[1]],
        pack_sum[4:8, cuts[1] : cuts[2]],
        pack_sum[4:8, cuts[2] : cuts[3]],
        pack_sum[9:11, 0:1],
        pack_sum[8, :narrow],
        dout_weight,
        pack_sum[3],
        dgate_weight.T,
        dup_weight.T,
        ddown_weight,
    )


def solution(mesh):
    rows = P(("dp", "tensor"), None)
    weight = P("dp", "tensor")
    channel = P(None, ("tensor", "dp"))
    down = P("tensor", "dp")
    return jax.shard_map(
        local,
        mesh=mesh,
        in_specs=(
            rows,
            P("dp", None),
            rows,
            P("dp"),
            weight,
            weight,
            weight,
            weight,
            weight,
            weight,
            channel,
            channel,
            channel,
            P(None, "tensor"),
            P(("tensor", "dp")),
            down,
            P("dp"),
            weight,
            weight,
            down,
        ),
        out_specs=(
            rows,
            rows,
            P("dp"),
            weight,
            weight,
            weight,
            weight,
            weight,
            weight,
            channel,
            channel,
            channel,
            P(None, "tensor"),
            P(("tensor", "dp")),
            down,
            P("dp"),
            weight,
            weight,
            down,
        ),
        check_vma=False,
    )
```
